256 devices in a mesh: section: 16 (over z_hi, x), tensor: 16 (over z_lo, y, core).
Axes of the slice: x: 4, y: 4, z: 8 (z_hi: 4, z_lo: 2; z = z_hi * 2 + z_lo), core: 2. Of those that a mesh axis runs over, the one named last changes fastest.
Arguments:
- hidden: bfloat16 [8192, 8192], P(('section', 'tensor')), may hold values from -2 to 2
- gain: float32 [16, 8192], P('section'), may hold values from 0.25 to 1.75
- w_query: bfloat16 [131072, 4096], P('section', 'tensor'), may hold values from -0.0625 to 0.0625
- w_keyval: bfloat16 [131072, 1024], P('section', 'tensor'), may hold values from -0.0625 to 0.0625
- w_out: bfloat16 [65536, 8192], P(('section', 'tensor')), may hold values from -0.09375 to 0.09375
- cache_kv: bfloat16 [24576, 1024], P('section', 'tensor'), may hold values from -360 to 360
- offsets: int32 [16], P('section'), may hold values from 0 to 1536, as said below
Outputs:
- handed: bfloat16 [8192, 8192], P(('section', 'tensor'))
The draws below stay inside these ranges and needn't reach their ends.
Inputs may be any that keep to these rules, and one draw needn't show every extreme that they name: `offsets`: each offset is a multiple of 512; some section has 1536 and some section has 0.
All inputs are finite; a program needn't handle non-finite values. Where the reference program divides by a largest or mean magnitude, that divisor is 1e-20 or more.
Results may differ from the reference program's by a relative error of at most 0.015.
The reference program's roundings to bfloat16 on the way count: a program that leaves them out, or rounds other values in their place, can miss the bound.
Values may be sent and summed in bfloat16 or wider, within the bound.
No kernel may reach another device: no remote copies, remote signals or barrier semaphores. Data moves between devices by JAX's collectives and lax.ppermute only.
A program may use at most 128 MiB of HBM per device.

```python
import math
import jax
import jax.numpy as jnp
from jax import lax

D = 8192
HD = 128
HEADS = 32
KVH = 4
BLOCK = 128
SPAN = 512
PRIOR = 3
CACHE = 1536
N_SECTION = 16
N_TENSOR = 16


def draw_offsets(key, part):
    key = jax.random.fold_in(key, 7)
    first, second, third = jax.random.split(key, 3)
    chosen = jax.random.randint(first, (N_SECTION,), 0, PRIOR + 1)
    fullest = jax.random.randint(second, (), 0, N_SECTION)
    emptiest = (fullest + 1 + jax.random.randint(third, (), 0, N_SECTION - 1)) % N_SECTION
    index = jnp.arange(N_SECTION, dtype=jnp.int32)
    chosen = jnp.where(index == fullest, PRIOR, chosen)
    chosen = jnp.where(index == emptiest, 0, chosen)
    return (chosen * SPAN).astype(jnp.int32)


def draw_cache_kv(key, part):
    key = jax.random.fold_in(key, 11)
    first = jax.random.fold_in(key, 0)
    third = jax.random.fold_in(key, 2)
    row_total = N_SECTION * CACHE
    width = KVH * HD
    keys = jnp.clip(jax.random.normal(first, (row_total, width), jnp.float32), -6.0, 6.0)
    vals = jnp.clip(jax.random.normal(third, (row_total, width), jnp.float32), -6.0, 6.0)
    return jnp.concatenate([keys, vals], axis=1).astype(jnp.bfloat16)


def level_of(stream_key, shape, shards, low, top_value):
    level = 1.0
    for axis_at, parts in shards:
        draws = jax.random.uniform(jax.random.fold_in(jax.random.fold_in(stream_key, 6), axis_at), (parts,), jnp.float32, low / len(shards), top_value / len(shards))
        level = level * jnp.repeat(jnp.exp(draws), shape[axis_at] // parts).reshape((-1,) + (1,) * (len(shape) - 1 - axis_at))
    return level


def normal_values(rng, extent, scale, reach, pieces=(), kind=jnp.bfloat16):
    drawn = jax.random.normal(rng, extent, jnp.float32) * scale
    if len(pieces) > 0:
        drawn = level_of(rng, extent, pieces, -0.22, 0.18) * drawn
    return jnp.clip(drawn, min=-reach, max=reach).astype(kind)


def setup_inputs(seed: int = 0) -> dict:
    key_of = jax.random.split(jax.random.key(seed), 8)
    return {
        "hidden": normal_values(key_of[0], (N_SECTION * SPAN, D), 0.25, 2.0, ((0, 256),)),
        "gain": jnp.clip(1.0 + 0.15 * jax.random.normal(key_of[1], (N_SECTION, D), jnp.float32), 0.25, 1.75),
        "w_query": normal_values(key_of[2], (N_SECTION * D, HEADS * HD), D ** -0.5, 0.0625, ((0, 16), (1, 16))),
        "w_keyval": normal_values(key_of[3], (N_SECTION * D, 2 * KVH * HD), D ** -0.5, 0.0625, ((0, 16), (1, 16))),
        "w_out": normal_values(key_of[4], (N_SECTION * HEADS * HD, D), (HEADS * HD) ** -0.5, 0.09375, ((0, 256),)),
        "cache_kv": draw_cache_kv(jax.random.fold_in(key_of[7], 71), 0),
        "offsets": draw_offsets(jax.random.fold_in(key_of[7], 71), 0),
    }


NORM_EPS = 1e-05
SCALE_EPS = 1e-06
ROPE_BASE = 500000.0

def rotation_table(size):
    index = jnp.arange(size, dtype=jnp.int32)
    common = index[:, None] & index[None, :]
    parity = jnp.zeros((size, size), jnp.int32)
    for bit in range(size.bit_length() - 1):
        parity = parity + (common >> bit & 1)
    signs = jnp.where(parity % 2 == 0, 1.0, -1.0).astype(jnp.float32)
    return signs / math.sqrt(size)

def rotary(values, positions, head_size):
    row_count = values.shape[0]
    heads = values.reshape(row_count, -1, head_size)
    half = head_size // 2
    freqs = ROPE_BASE ** (-(2.0 / head_size) * jnp.arange(half, dtype=jnp.float32))
    angles = positions.astype(jnp.float32)[:, None] * freqs[None, :]
    cosine = jnp.cos(angles)[:, None, :]
    sine = jnp.sin(angles)[:, None, :]
    first = heads[..., :half]
    second = heads[..., half:]
    turned = jnp.concatenate([first * cosine - second * sine, second * cosine + first * sine], axis=-1)
    return turned.reshape(row_count, -1)

def normalize(hidden, gain):
    values = hidden.astype(jnp.float32)
    inverse = lax.rsqrt(lax.optimization_barrier(jnp.mean(values * values, axis=-1, keepdims=True)) + NORM_EPS)
    return (values, (values * inverse * gain[None, :]).astype(jnp.bfloat16))

def attend(query, keys, values, visible):
    scores = lax.dot_general(query, keys, (((1,), (1,)), ((), ())), preferred_element_type=jnp.float32)
    scores = jnp.where(visible, scores / math.sqrt(HD), -1e+30)
    highest = lax.optimization_barrier(jnp.max(scores, axis=-1, keepdims=True))
    raised = jnp.exp(scores - highest)
    weights = (raised / lax.optimization_barrier(jnp.sum(raised, axis=-1, keepdims=True))).astype(jnp.bfloat16)
    return jnp.dot(weights, values, preferred_element_type=jnp.float32).astype(jnp.bfloat16)

def quantize(partial_value, table):
    blocks = partial_value.reshape(partial_value.shape[0], -1, BLOCK)
    turned = jnp.einsum('rnb,bc->rnc', blocks, table, precision=lax.Precision.HIGHEST)
    scales = lax.optimization_barrier(jnp.max(jnp.abs(turned), axis=-1)) + SCALE_EPS
    levels = (turned / scales[..., None]).astype(jnp.bfloat16)
    return (levels, scales)

def section_layer(operands):
    hidden, gain, w_query, w_keyval, w_out, cache, offset = operands
    values, normed = normalize(hidden, gain)
    positions = offset + jnp.arange(SPAN, dtype=jnp.int32)
    query = rotary(jnp.dot(normed, w_query, preferred_element_type=jnp.float32), positions, HD).astype(jnp.bfloat16)
    keyval = jnp.dot(normed, w_keyval, preferred_element_type=jnp.float32).astype(jnp.bfloat16)
    width = KVH * HD
    new_keys = rotary(keyval[:, :width].astype(jnp.float32), positions, HD).astype(jnp.bfloat16)
    keys = jnp.concatenate([cache[:, :width], new_keys], axis=0)
    vals = jnp.concatenate([cache[:, width:], keyval[:, width:]], axis=0)
    key_index = jnp.arange(CACHE + SPAN, dtype=jnp.int32)[None, :]
    query_index = jnp.arange(SPAN, dtype=jnp.int32)[:, None]
    visible = jnp.where(key_index < CACHE, key_index < offset, key_index - CACHE <= query_index)
    group = HEADS // KVH
    outputs = []
    for head_index in range(HEADS):
        source = head_index // group
        outputs.append(attend(query[:, head_index * HD:(head_index + 1) * HD], keys[:, source * HD:(source + 1) * HD], vals[:, source * HD:(source + 1) * HD], visible))
    attention = jnp.concatenate(outputs, axis=1)
    table = rotation_table(BLOCK)
    per_group = HEADS * HD // N_TENSOR

    def accumulate(total, index):
        piece = lax.dynamic_slice_in_dim(attention, index * per_group, per_group, 1)
        weight = lax.dynamic_slice_in_dim(w_out, index * per_group, per_group, 0)
        levels, scales = quantize(jnp.dot(piece, weight, preferred_element_type=jnp.float32), table)
        return (total + scales[..., None] * levels.astype(jnp.float32), None)
    start = jnp.zeros((SPAN, D // BLOCK, BLOCK), jnp.float32)
    total, unused = lax.scan(accumulate, start, jnp.arange(N_TENSOR, dtype=jnp.int32))
    restored = jnp.einsum('rnb,bc->rnc', total, table, precision=lax.Precision.HIGHEST).reshape(SPAN, D)
    return (values + restored).astype(jnp.bfloat16)

def reference(hidden, gain, w_query, w_keyval, w_out, cache_kv, offsets):
    stacked = (hidden.reshape(N_SECTION, SPAN, D), gain, w_query.reshape(N_SECTION, D, HEADS * HD), w_keyval.reshape(N_SECTION, D, 2 * KVH * HD), w_out.reshape(N_SECTION, HEADS * HD, D), cache_kv.reshape(N_SECTION, CACHE, 2 * KVH * HD), offsets)
    layers = lax.map(section_layer, stacked)
    return jnp.roll(layers, 1, axis=0).reshape(N_SECTION * SPAN, D)
```

```python
import functools
import math

import jax
import jax.numpy as jnp
from jax import lax
from jax.experimental import pallas as pl
from jax.experimental.pallas import tpu as pltpu
from jax.sharding import PartitionSpec as P

HD = 128
HEADS = 32
KVH = 4
BLOCK = 128
GROUP = 16
ROWS = 32
SPAN = 512
CHUNKS = 2

NORM_EPS = 1e-05
SCALE_EPS = 1e-06
ROPE_BASE = 500000.0
F32 = jnp.float32
BF16 = jnp.bfloat16


def send(block, target):
    return lax.ppermute(block, "tensor", [(t, target(t)) for t in range(GROUP)])


def by_y(distance):
    return lambda t: (t & 9) | ((((t >> 1) + distance) & 3) << 1)


def by_z(t):
    return t ^ 8


def by_core(t):
    return t ^ 1


STEPS = [(0, 0), (0, 1), (0, 3), (0, 2), (1, 0), (1, 1), (1, 3), (1, 2)]


def seen_from(position):
    z, y, core = position >> 3, (position >> 1) & 3, position & 1
    same = jnp.stack([((z ^ dz) << 3) | (((y + dy) & 3) << 1) | core for dz, dy in STEPS])
    return same, same ^ 1


def hadamard(size):
    index = jnp.arange(size, dtype=jnp.int32)
    common = index[:, None] & index[None, :]
    parity = jnp.zeros((size, size), jnp.int32)
    for bit in range(size.bit_length() - 1):
        parity = parity + (common >> bit & 1)
    return jnp.where(parity % 2 == 0, 1.0, -1.0).astype(F32)


def rotary(values, positions):
    row_count = values.shape[0]
    heads = values.reshape(row_count, -1, HD)
    half = HD // 2
    freqs = ROPE_BASE ** (-(2.0 / HD) * jnp.arange(half, dtype=F32))
    angles = positions.astype(F32)[:, None] * freqs[None, :]
    cosine = jnp.cos(angles)[:, None, :]
    sine = jnp.sin(angles)[:, None, :]
    first = heads[..., :half]
    second = heads[..., half:]
    turned = jnp.concatenate(
        [first * cosine - second * sine, second * cosine + first * sine], axis=-1
    )
    return turned.reshape(row_count, -1)


def project_kernel(layout, step, *refs):
    count = len(refs) - 4
    pieces, (wq_ref, wkv_ref, q_ref, kv_ref) = refs[:count], refs[count:]
    width = wq_ref.shape[0]
    q = jnp.zeros(q_ref.shape, F32)
    kv = jnp.zeros(kv_ref.shape, F32)
    for start in range(0, width, step):
        parts = []
        for spans in layout:
            for which, low, high, base in spans:
                if low <= start < high:
                    parts.append(pieces[which][:, base + start - low : base + start - low + step])
        rows = jnp.concatenate(parts, axis=0)
        q += jnp.dot(rows, wq_ref[start : start + step, :], preferred_element_type=F32)
        kv += jnp.dot(rows, wkv_ref[start : start + step, :], preferred_element_type=F32)
    q_ref[...] = q
    kv_ref[...] = kv


def project(pieces, layout, w_query, w_keyval, step=1024):
    rows = ROWS * len(layout)
    return pl.pallas_call(
        functools.partial(project_kernel, layout, step),
        out_shape=(
            jax.ShapeDtypeStruct((rows, w_query.shape[1]), F32),
            jax.ShapeDtypeStruct((rows, w_keyval.shape[1]), F32),
        ),
        compiler_params=pltpu.CompilerParams(vmem_limit_bytes=48 << 20),
        cost_estimate=pl.CostEstimate(
            flops=2 * rows * w_query.shape[0] * 320, bytes_accessed=9 << 20, transcendentals=0
        ),
    )(*pieces, w_query, w_keyval)


def output_kernel(att_ref, w_ref, table_ref, keep_ref, give_ref):
    part = jnp.dot(att_ref[...], w_ref[...], preferred_element_type=F32)
    root = 1.0 / math.sqrt(BLOCK)
    half = keep_ref.shape[0]
    for start in range(0, part.shape[1], 2 * BLOCK):
        piece = part[:, start : start + 2 * BLOCK]
        high = piece.astype(BF16)
        low = (piece - high.astype(F32)).astype(BF16)
        turned = jnp.dot(high, table_ref[...], preferred_element_type=F32)
        turned += jnp.dot(low, table_ref[...], preferred_element_type=F32)
        for at in range(0, 2 * BLOCK, BLOCK):
            block = turned[:, at : at + BLOCK] * root
            scale = jnp.max(jnp.abs(block), axis=1, keepdims=True) + SCALE_EPS
            level = (block / scale).astype(BF16)
            value = scale * level.astype(F32)
            columns = slice(start + at, start + at + BLOCK)
            keep_ref[:, columns] = value[:half]
            give_ref[:, columns] = value[half:].astype(BF16)


def output_partial(attention, w_out, table, chunk, tile=512):
    rows, depth = attention.shape
    width = w_out.shape[1] // CHUNKS
    steps = width // tile
    return pl.pallas_call(
        output_kernel,
        grid=(steps,),
        in_specs=[
            pl.BlockSpec((rows, depth), lambda i: (0, 0)),
            pl.BlockSpec((depth, tile), lambda i: (0, chunk * steps + i)),
            pl.BlockSpec(table.shape, lambda i: (0, 0)),
        ],
        out_specs=(
            pl.BlockSpec((rows // 2, tile), lambda i: (0, i)),
            pl.BlockSpec((rows // 2, tile), lambda i: (0, i)),
        ),
        out_shape=(
            jax.ShapeDtypeStruct((rows // 2, width), F32),
            jax.ShapeDtypeStruct((rows // 2, width), BF16),
        ),
        compiler_params=pltpu.CompilerParams(vmem_limit_bytes=48 << 20),
        cost_estimate=pl.CostEstimate(
            flops=2 * rows * width * 768, bytes_accessed=10 << 20, transcendentals=0
        ),
    )(attention, w_out, table)


def attend(query, keys, values, visible):
    scores = lax.dot_general(query, keys, (((1,), (1,)), ((), ())), preferred_element_type=F32)
    scores = jnp.where(visible, scores / math.sqrt(HD), -1e30)
    highest = jnp.max(scores, axis=-1, keepdims=True)
    raised = jnp.exp(scores - highest)
    weights = (raised / jnp.sum(raised, axis=-1, keepdims=True)).astype(BF16)
    return jnp.dot(weights, values, preferred_element_type=F32).astype(BF16)


def head_columns(block, position):
    mine = position & 3
    got = []
    for turn in range(4):
        pairs = []
        for t in range(GROUP):
            head, i = t >> 2, t & 3
            sources = [2 * head, 2 * head + 1, 8 + 2 * head, 9 + 2 * head]
            pairs.append((sources[(i + turn) & 3], t))
        got.append(lax.ppermute(block, "tensor", pairs))
    got = jnp.stack(got)
    order = (jnp.arange(4, dtype=jnp.int32) - mine) & 3
    got = jnp.take(got, order, axis=0)
    return jnp.concatenate([got[0], got[1]], axis=1), jnp.concatenate([got[2], got[3]], axis=1)


def reduce_chunk(keep, give, width):
    got = send(give, by_core)
    total = (keep + got.astype(F32)).reshape(8, ROWS, width)
    own, up, down, far, other, o_up, o_down, o_far = [total[i] for i in range(8)]
    half, quarter = width // 2, width // 4
    to_up = jnp.concatenate([far[:, :half], o_up[:, :quarter]], axis=1).astype(BF16)
    to_down = jnp.concatenate([far[:, half:], o_down[:, :quarter]], axis=1).astype(BF16)
    to_z = jnp.concatenate([o_up[:, quarter:], o_down[:, quarter:]], axis=1).astype(BF16)
    from_far = send(o_far.astype(BF16), by_y(2)).astype(F32)
    from_down = send(to_up, by_y(1)).astype(F32)
    from_up = send(to_down, by_y(-1)).astype(F32)
    from_z = send(to_z, by_z).astype(F32)
    rest = width - quarter
    up = up + jnp.pad(from_down[:, :half], ((0, 0), (0, half)))
    up = up + jnp.pad(from_z[:, :rest], ((0, 0), (quarter, 0)))
    down = down + jnp.pad(from_up[:, :half], ((0, 0), (half, 0)))
    down = down + jnp.pad(from_z[:, rest:], ((0, 0), (quarter, 0)))
    other = other + from_far
    other = other + jnp.pad(from_down[:, half:] + from_up[:, half:], ((0, 0), (0, rest)))
    last = send(up.astype(BF16), by_y(1)).astype(F32)
    last = last + send(down.astype(BF16), by_y(-1)).astype(F32)
    last = last + send(other.astype(BF16), by_z).astype(F32)
    return own + last


def local(hidden, gain, w_query, w_keyval, w_out, cache_kv, offsets):
    position = lax.axis_index("tensor")
    offset = offsets[0]
    values = hidden.astype(F32)
    inverse = lax.rsqrt(jnp.mean(values * values, axis=-1, keepdims=True) + NORM_EPS)
    normed = (values * inverse * gain[0][None, :]).astype(BF16)

    up = send(normed, by_y(-1))
    down = send(normed, by_y(1))
    other = send(normed, by_z)
    near = [normed, up, down, other]
    near = near + [send(piece, by_core) for piece in near]
    cache_keys, cache_values = head_columns(cache_kv, position)
    half, quarter = 4096, 2048
    from_up = send(jnp.concatenate([up[:, :half], other[:, :quarter]], axis=1), by_y(-1))
    from_down = send(jnp.concatenate([down[:, half:], other[:, :quarter]], axis=1), by_y(1))
    from_z = send(jnp.concatenate([up[:, quarter:], down[:, quarter:]], axis=1), by_z)
    far = send(other, by_y(2))
    distant = [from_up, from_down, from_z, far]
    distant = distant + [send(piece, by_core) for piece in distant]

    full = 8192
    near_layout = [[(i, 0, full, 0)] for i in range(8)]
    far_layout = []
    for base in (0, 4):
        far_layout += [
            [(base, 0, half, 0), (base + 1, half, full, 0)],
            [(base, 0, quarter, half), (base + 2, quarter, full, 0)],
            [(base + 1, 0, quarter, half), (base + 2, quarter, full, full - quarter)],
            [(base + 3, 0, full, 0)],
        ]
    q_near, kv_near = project(near, near_layout, w_query, w_keyval)
    q_far, kv_far = project(distant, far_layout, w_query, w_keyval)

    same, cross = seen_from(position)
    first, second = jnp.array([0, 1, 2, 4]), jnp.array([3, 5, 6, 7])
    held = jnp.concatenate([same[first], cross[first], same[second], cross[second]])
    place = jnp.argsort(held)

    def in_order(near_part, far_part):
        both = jnp.concatenate([near_part, far_part], axis=0).reshape(GROUP, ROWS, -1)
        return jnp.take(both, place, axis=0).reshape(SPAN, -1)

    keyval = in_order(kv_near, kv_far).astype(BF16)
    new_keys, new_values = head_columns(keyval, position)
    positions = offset + jnp.arange(SPAN, dtype=jnp.int32)
    query = rotary(in_order(q_near, q_far), positions).astype(BF16)
    new_keys = rotary(new_keys.astype(F32), positions).astype(BF16)
    keys = jnp.concatenate([cache_keys, new_keys], axis=0)
    vals = jnp.concatenate([cache_values, new_values], axis=0)
    cache_rows = cache_kv.shape[0]
    key_index = jnp.arange(cache_rows + SPAN, dtype=jnp.int32)[None, :]
    query_index = jnp.arange(SPAN, dtype=jnp.int32)[:, None]
    visible = jnp.where(
        key_index < cache_rows, key_index < offset, key_index - cache_rows <= query_index
    )
    attention = jnp.concatenate(
        [attend(query[:, at : at + HD], keys, vals, visible) for at in (0, HD)], axis=1
    )
    aim = jnp.concatenate([same, cross])
    attention = jnp.take(attention.reshape(GROUP, ROWS, -1), aim, axis=0).reshape(SPAN, -1)

    table = hadamard(BLOCK)
    zero = jnp.zeros_like(table)
    pair = jnp.concatenate(
        [jnp.concatenate([table, zero], axis=1), jnp.concatenate([zero, table], axis=1)], axis=0
    ).astype(BF16)
    width = w_out.shape[1] // CHUNKS
    results = []
    for chunk in range(CHUNKS):
        keep, give = output_partial(attention, w_out, pair, chunk)
        total = reduce_chunk(keep, give, width)
        restored = jnp.einsum(
            "rnb,bc->rnc",
            total.reshape(ROWS, -1, BLOCK),
            table / math.sqrt(BLOCK),
            precision=lax.Precision.HIGHEST,
        ).reshape(ROWS, width)
        layer = (values[:, chunk * width : (chunk + 1) * width] + restored).astype(BF16)
        sections = lax.axis_size("section")
        route = [(i, (i + 1) % sections) for i in range(sections)]
        results.append(lax.ppermute(layer, "section", route))
    return jnp.concatenate(results, axis=1)


def solution(mesh):
    placed = (
        P(("section", "tensor"), None),
        P("section", None),
        P("section", "tensor"),
        P("section", "tensor"),
        P(("section", "tensor"), None),
        P("section", "tensor"),
        P("section"),
    )
    return jax.shard_map(
        local, mesh=mesh, in_specs=placed, out_specs=P(("section", "tensor"), None), check_vma=False
    )
```

```python
import functools
import math

import jax
import jax.numpy as jnp
from jax import lax
from jax.experimental import pallas as pl
from jax.experimental.pallas import tpu as pltpu
from jax.sharding import PartitionSpec as P

HD = 128
HEADS = 32
KVH = 4
BLOCK = 128
GROUP = 16
ROWS = 32
SPAN = 512
CHUNKS = (2560, 3072, 2560)

NORM_EPS = 1e-05
SCALE_EPS = 1e-06
ROPE_BASE = 500000.0
F32 = jnp.float32
BF16 = jnp.bfloat16


def send(block, target):
    return lax.ppermute(block, "tensor", [(t, target(t)) for t in range(GROUP)])


def by_y(distance):
    return lambda t: (t & 9) | ((((t >> 1) + distance) & 3) << 1)


def by_z(t):
    return t ^ 8


def by_core(t):
    return t ^ 1


NEAR = [(0, 0), (0, 1), (0, 3), (1, 0)]
FAR = [(0, 2), (1, 1), (1, 3), (1, 2)]
ROWS_BY_ROWS = (((1,), (1,)), ((), ()))
NO_COST = pl.CostEstimate(flops=0, bytes_accessed=0, transcendentals=0)
VMEM = pl.BlockSpec(memory_space=pltpu.VMEM)
SMEM = pl.BlockSpec(memory_space=pltpu.SMEM)


def held_rows(position):
    z, y, core = position >> 3, (position >> 1) & 3, position & 1
    blocks = [
        ((z ^ dz) << 3) | (((y + dy) & 3) << 1) | (core ^ swap)
        for steps in (NEAR, FAR)
        for swap in (0, 1)
        for dz, dy in steps
    ]
    return (jnp.stack(blocks)[:, None] * ROWS + jnp.arange(ROWS, dtype=jnp.int32)).reshape(-1)


def hadamard(size):
    index = jnp.arange(size, dtype=jnp.int32)
    common = index[:, None] & index[None, :]
    parity = jnp.zeros((size, size), jnp.int32)
    for bit in range(size.bit_length() - 1):
        parity = parity + (common >> bit & 1)
    return jnp.where(parity % 2 == 0, 1.0, -1.0).astype(F32)


def call(kernel, shapes, inputs, scalars=(), behind=(), limit=12, scratch=()):
    count, waits = len(inputs), len(behind)
    specs = [SMEM if i in scalars else VMEM for i in range(count)]

    def body(*refs):
        kernel(*refs[:count], *refs[count + waits :])

    return pl.pallas_call(
        body,
        out_shape=shapes,
        in_specs=specs + [pl.BlockSpec(memory_space=pl.ANY)] * waits,
        out_specs=jax.tree.map(lambda _: VMEM, shapes),
        scratch_shapes=scratch,
        compiler_params=pltpu.CompilerParams(vmem_limit_bytes=limit << 20),
        cost_estimate=NO_COST,
    )(*inputs, *behind)


def shape(rows, columns, kind=BF16):
    return jax.ShapeDtypeStruct((rows, columns), kind)


def norm_kernel(x_ref, gain_ref, out_ref):
    values = x_ref[...].astype(F32)
    inverse = lax.rsqrt(jnp.mean(values * values, axis=1, keepdims=True) + NORM_EPS)
    out_ref[...] = (values * inverse * gain_ref[...]).astype(BF16)


def forward_kernel(own_ref, up_ref, down_ref, other_ref, to_down_ref, to_up_ref, to_z_ref, near_ref):
    full = own_ref.shape[1]
    half, quarter = full // 2, full // 4
    to_down_ref[:, :half] = up_ref[:, :half]
    to_down_ref[:, half:] = other_ref[:, :quarter]
    to_up_ref[:, :half] = down_ref[:, half:]
    to_up_ref[:, half:] = other_ref[:, :quarter]
    to_z_ref[:, : full - quarter] = up_ref[:, quarter:]
    to_z_ref[:, full - quarter :] = down_ref[:, quarter:]
    for place, ref in enumerate((own_ref, up_ref, down_ref, other_ref)):
        near_ref[place * ROWS : (place + 1) * ROWS, :] = ref[...]


def copy_kernel(in_ref, out_ref):
    out_ref[...] = in_ref[...]


def join_kernel(*refs):
    out_ref, at = refs[-1], 0
    for top, low in (refs[:2], refs[2:4]):
        rows, width = top.shape
        out_ref[:rows, at : at + width] = top[...]
        out_ref[rows:, at : at + width] = low[...]
        at += width


def near_kernel(step, mine_ref, theirs_ref, wq_ref, wkv_ref, q_ref, kv_ref):
    q = jnp.zeros(q_ref.shape, F32)
    kv = jnp.zeros(kv_ref.shape, F32)
    for start in range(0, wq_ref.shape[0], step):
        at = slice(start, start + step)
        rows = jnp.concatenate([mine_ref[:, at], theirs_ref[:, at]], axis=0)
        q += jnp.dot(rows, wq_ref[at, :], preferred_element_type=F32)
        kv += lax.dot_general(wkv_ref[:, at], rows, ROWS_BY_ROWS, preferred_element_type=F32)
    q_ref[...] = q
    kv_ref[...] = kv.astype(BF16)


def gathered(layout, pieces, start, step):
    parts = []
    for spans in layout:
        for which, low, high, base in spans:
            if low <= start < high:
                parts.append(pieces[which][:, base + start - low : base + start - low + step])
    return jnp.concatenate(parts, axis=0)


def far_keyval_kernel(layout, step, *refs):
    pieces, (wkv_ref, near_ref, order_ref, kv_ref) = refs[:-4], refs[-4:]
    kv = jnp.zeros(near_ref.shape, F32)
    for start in range(0, wkv_ref.shape[1], step):
        rows = gathered(layout, pieces, start, step)
        columns = wkv_ref[:, start : start + step]
        kv += lax.dot_general(columns, rows, ROWS_BY_ROWS, preferred_element_type=F32)
    both = jnp.concatenate([near_ref[...], kv.astype(BF16)], axis=1)
    kv_ref[...] = jnp.dot(both, order_ref[...], preferred_element_type=F32).astype(BF16)


def far_query_kernel(layout, step, *refs):
    pieces, (wq_ref, q_ref) = refs[:-2], refs[-2:]
    q = jnp.zeros(q_ref.shape, F32)
    for start in range(0, wq_ref.shape[0], step):
        rows = gathered(layout, pieces, start, step)
        q += jnp.dot(rows, wq_ref[start : start + step, :], preferred_element_type=F32)
    q_ref[...] = q


def pick(flags_ref, mine, theirs):
    half = mine.shape[0] // 2
    turned, core = flags_ref[0] != 0, flags_ref[1] != 0
    low = jnp.where(core, theirs, mine)
    high = jnp.where(core, mine, theirs)
    keys = jnp.concatenate(
        [jnp.where(turned, low[half:], low[:half]), jnp.where(turned, high[half:], high[:half])]
    )
    values = jnp.concatenate(
        [jnp.where(turned, low[:half], low[half:]), jnp.where(turned, high[:half], high[half:])]
    )
    return keys, values


TILE = 256


def attend_kernel(cached, flags_ref, qn_ref, qf_ref, row_ref, key_ref, mine_ref, theirs_ref, out_ref, joined_ref):
    keys, values = pick(flags_ref, mine_ref[...], theirs_ref[...])
    half = HD // 2
    first, second = keys[:half, cached:].astype(F32), keys[half:, cached:].astype(F32)
    cosine, sine = key_ref[:half, :], key_ref[half:, :]
    new_keys = jnp.concatenate(
        [first * cosine - second * sine, second * cosine + first * sine], axis=0
    ).astype(BF16)
    old_keys, old_values, new_values = keys[:, :cached], values[:, :cached], values[:, cached:]
    bias = jnp.where(
        lax.broadcasted_iota(jnp.int32, (1, cached), 1) < flags_ref[2], 0.0, -1e30
    )
    factor = 1.0 / math.sqrt(HD)
    for source, start in ((qn_ref, 0), (qf_ref, TILE)):
        at = slice(start, start + TILE)
        column = lax.broadcasted_iota(jnp.int32, (TILE, new_keys.shape[1]), 1)
        seen = column <= row_ref[at, 2 * HD : 2 * HD + 1].astype(jnp.int32)
        for head in range(2):
            columns = slice(head * HD, (head + 1) * HD)
            raw = source[:, columns]
            query = raw * row_ref[at, :HD] + pltpu.roll(raw, half, 1) * row_ref[at, HD : 2 * HD]
            query = query.astype(BF16)
            old = jnp.dot(query, old_keys, preferred_element_type=F32) * factor + bias
            new = jnp.dot(query, new_keys, preferred_element_type=F32) * factor
            new = jnp.where(seen, new, -1e30)
            top = jnp.maximum(
                jnp.max(old, axis=1, keepdims=True), jnp.max(new, axis=1, keepdims=True)
            )
            old, new = jnp.exp(old - top), jnp.exp(new - top)
            total = jnp.sum(old, axis=1, keepdims=True) + jnp.sum(new, axis=1, keepdims=True)
            value = lax.dot_general(
                old.astype(BF16), old_values, ROWS_BY_ROWS, preferred_element_type=F32
            )
            value += lax.dot_general(
                new.astype(BF16), new_values, ROWS_BY_ROWS, preferred_element_type=F32
            )
            joined_ref[at, columns] = (value / total).astype(BF16)
    for core in (0, 1):
        near, far = 4 * core, 8 + 4 * core
        order = (near, near + 3, near + 1, far + 1, near + 2, far + 2, far, far + 3)
        for place, block in enumerate(order):
            piece = joined_ref[block * ROWS : (block + 1) * ROWS, :]
            to = slice((8 * core + place) * ROWS, (8 * core + place + 1) * ROWS)
            out_ref[to, : 2 * HD] = piece
            out_ref[to, 2 * HD :] = piece


def turn_kernel(w_ref, table_ref, out_ref):
    rows = w_ref.shape[0]
    for start in range(0, w_ref.shape[1], 2 * BLOCK):
        at = slice(start, start + 2 * BLOCK)
        turned = jnp.dot(w_ref[:, at], table_ref[...], preferred_element_type=F32)
        turned = turned * (1.0 / math.sqrt(BLOCK))
        high = turned.astype(BF16)
        out_ref[:rows, at] = high
        out_ref[rows:, at] = (turned - high.astype(F32)).astype(BF16)


def turn_weights(w_out, table, start, width, behind, tile=512):
    rows = w_out.shape[0]
    return pl.pallas_call(
        lambda w_ref, table_ref, behind_ref, out_ref: turn_kernel(w_ref, table_ref, out_ref),
        grid=(width // tile,),
        in_specs=[
            pl.BlockSpec((rows, tile), lambda i: (0, start // tile + i)),
            pl.BlockSpec(table.shape, lambda i: (0, 0)),
            pl.BlockSpec(memory_space=pl.ANY),
        ],
        out_specs=pl.BlockSpec((2 * rows, tile), lambda i: (0, i)),
        out_shape=jax.ShapeDtypeStruct((2 * rows, width), BF16),
        compiler_params=pltpu.CompilerParams(vmem_limit_bytes=8 << 20),
        cost_estimate=NO_COST,
    )(w_out, table, behind)


def output_kernel(att_ref, w_ref, keep_ref, give_ref):
    half = keep_ref.shape[0]
    for start in range(0, w_ref.shape[1], 2 * BLOCK):
        pair = jnp.dot(
            att_ref[...], w_ref[:, start : start + 2 * BLOCK], preferred_element_type=F32
        )
        for at in range(0, 2 * BLOCK, BLOCK):
            block = pair[:, at : at + BLOCK]
            scale = jnp.max(jnp.abs(block), axis=1, keepdims=True) + SCALE_EPS
            level = (block * (1.0 / scale)).astype(BF16)
            value = (scale * level.astype(F32)).astype(BF16)
            columns = slice(start + at, start + at + BLOCK)
            keep_ref[:, columns] = value[:half]
            give_ref[:, columns] = value[half:]


def output_partial(attention, turned, behind=(), tile=512):
    rows, depth = attention.shape
    width = turned.shape[1]
    half, waits = shape(rows // 2, width), len(behind)
    return pl.pallas_call(
        lambda *refs: output_kernel(*refs[:2], *refs[2 + waits :]),
        grid=(width // tile,),
        in_specs=[
            pl.BlockSpec((rows, depth), lambda i: (0, 0)),
            pl.BlockSpec((depth, tile), lambda i: (0, i)),
        ]
        + [pl.BlockSpec(memory_space=pl.ANY)] * waits,
        out_specs=(
            pl.BlockSpec((rows // 2, tile), lambda i: (0, i)),
            pl.BlockSpec((rows // 2, tile), lambda i: (0, i)),
        ),
        out_shape=(half, half),
        compiler_params=pltpu.CompilerParams(vmem_limit_bytes=10 << 20),
        cost_estimate=pl.CostEstimate(
            flops=5000000 * width, bytes_accessed=0, transcendentals=0
        ),
    )(attention, turned, *behind)


def gather_head(block):
    got = []
    for turn in range(2):
        pairs = []
        for t in range(GROUP):
            head, chip, core = t >> 2, (t >> 1) & 1, t & 1
            pairs.append((8 * (chip ^ turn) + 2 * head + core, t))
        got.append(lax.ppermute(block, "tensor", pairs))
    return got


def add_kernel(keep_ref, got_ref, to_up_ref, to_down_ref, rest_ref):
    half = to_up_ref.shape[1] // 2
    left, right = slice(0, half), slice(half, 2 * half)

    def total(first, last, columns):
        return keep_ref[first:last, columns].astype(F32) + got_ref[first:last, columns].astype(F32)

    to_up_ref[:, left] = total(192, 256, left).astype(BF16)
    to_up_ref[:, right] = total(64, 128, right).astype(BF16)
    to_down_ref[:, left] = total(128, 192, left).astype(BF16)
    to_down_ref[:, right] = total(192, 256, right).astype(BF16)
    rest_ref[:64, left] = total(0, 64, left)
    rest_ref[:64, right] = total(0, 64, right)
    rest_ref[64:, left] = total(64, 128, left)
    rest_ref[64:, right] = total(128, 192, right)


def middle_kernel(rest_ref, from_down_ref, from_up_ref, to_up_ref, to_down_ref, near_ref):
    half = to_up_ref.shape[1]
    left, right = slice(0, half), slice(half, 2 * half)
    to_up_ref[...] = (rest_ref[64:, left] + from_down_ref[:, left].astype(F32)).astype(BF16)
    to_down_ref[...] = (rest_ref[64:, right] + from_up_ref[:, right].astype(F32)).astype(BF16)
    near_ref[:, left] = rest_ref[:64, left] + from_up_ref[:, left].astype(F32)
    near_ref[:, right] = rest_ref[:64, right] + from_down_ref[:, right].astype(F32)


def last_kernel(near_ref, from_down_ref, from_up_ref, mine_ref, to_z_ref):
    half = from_up_ref.shape[1]
    for at, ref in ((0, from_down_ref), (half, from_up_ref)):
        columns = slice(at, at + half)
        total = near_ref[:, columns] + ref[...].astype(F32)
        mine_ref[:, columns] = total[:32]
        to_z_ref[:, columns] = total[32:].astype(BF16)


def layer_kernel(start, mine_ref, from_z_ref, hidden_ref, table_ref, out_ref):
    total = mine_ref[...] + from_z_ref[...].astype(F32)
    for at in range(0, total.shape[1], 2 * BLOCK):
        rest = total[:, at : at + 2 * BLOCK]
        restored = jnp.zeros(rest.shape, F32)
        for _ in range(3):
            part = rest.astype(BF16)
            restored += jnp.dot(part, table_ref[...], preferred_element_type=F32)
            rest = rest - part.astype(F32)
        before = hidden_ref[:, start + at : start + at + 2 * BLOCK].astype(F32)
        out_ref[:, at : at + 2 * BLOCK] = (before + restored * (1.0 / math.sqrt(BLOCK))).astype(BF16)


def local(hidden, gain, w_query, w_keyval, w_out, cache_kv, offsets):
    position = lax.axis_index("tensor")
    offset = offsets[0]
    full = w_query.shape[0]
    normed = call(norm_kernel, shape(*hidden.shape), (hidden, gain))

    up = send(normed, by_y(-1))
    down = send(normed, by_y(1))
    other = send(normed, by_z)

    held = held_rows(position)
    span = jnp.arange(SPAN, dtype=jnp.int32)
    order = (held[:, None] == span[None, :]).astype(BF16)
    freqs = ROPE_BASE ** (-(2.0 / HD) * jnp.arange(HD // 2, dtype=F32))
    angles = (offset + held).astype(F32)[:, None] * freqs[None, :]
    cosine, sine = jnp.cos(angles), jnp.sin(angles)
    index = jnp.broadcast_to(held.astype(F32)[:, None], (SPAN, HD))
    row_table = jnp.concatenate([cosine, cosine, -sine, sine, index], axis=1)
    angles = freqs[:, None] * (offset + span).astype(F32)[None, :]
    key_table = jnp.concatenate([jnp.cos(angles), jnp.sin(angles)], axis=0)
    flags = jnp.stack([(position >> 1) & 1, position & 1, offset]).astype(jnp.int32)
    table = hadamard(BLOCK)
    zero = jnp.zeros_like(table)
    pair = jnp.concatenate(
        [jnp.concatenate([table, zero], axis=1), jnp.concatenate([zero, table], axis=1)], axis=0
    ).astype(BF16)
    starts = [sum(CHUNKS[:i]) for i in range(len(CHUNKS))]

    half, quarter = full // 2, full // 4
    to_down, to_up, to_z, near = call(
        forward_kernel,
        (shape(ROWS, half + quarter), shape(ROWS, half + quarter), shape(ROWS, 2 * (full - quarter)), shape(4 * ROWS, full)),
        (normed, up, down, other),
        behind=(order, row_table, key_table, pair),
    )
    from_up = send(to_down, by_y(-1))
    from_down = send(to_up, by_y(1))
    from_z = send(to_z, by_z)
    far = send(other, by_y(2))
    near_theirs = send(near, by_core)
    turned = [turn_weights(w_out, pair, at, width, to_z) for at, width in zip(starts, CHUNKS)]
    layout = []
    for base in (0, 4):
        layout += [
            [(base, 0, half, 0), (base + 1, half, full, 0)],
            [(base, 0, quarter, half), (base + 2, quarter, full, 0)],
            [(base + 1, 0, quarter, half), (base + 2, quarter, full, full - quarter)],
            [(base + 3, 0, full, 0)],
        ]
    query_width, kv_width = w_query.shape[1], w_keyval.shape[1]
    rows, cached = SPAN // 2, cache_kv.shape[0]
    q_near, kv_near = call(
        functools.partial(near_kernel, 1024),
        (shape(rows, query_width, F32), shape(kv_width, rows)),
        (near, near_theirs, w_query, w_keyval.T),
        behind=turned,
    )
    distant = [from_up, from_down, from_z, far]
    cache = call(copy_kernel, shape(kv_width, cached), (cache_kv.T,), behind=distant)
    from_z = call(copy_kernel, shape(*from_z.shape), (from_z,), behind=(kv_near,))
    distant = distant + [send(piece, by_core) for piece in (from_up, from_down, from_z, far)]
    cache = gather_head(cache)
    keyval = call(
        functools.partial(far_keyval_kernel, layout, 1024),
        shape(kv_width, SPAN),
        (*distant, w_keyval.T, kv_near, order),
    )
    new = gather_head(keyval)
    q_far = call(
        functools.partial(far_query_kernel, layout, 1024),
        shape(rows, query_width, F32),
        (*distant, w_query),
        behind=(keyval,),
    )
    mine = call(join_kernel, shape(2 * kv_width, cached + SPAN), (*cache, *new), behind=(q_far,))
    attention = call(
        functools.partial(attend_kernel, cached),
        shape(SPAN, 2 * query_width),
        (flags, q_near, q_far, row_table, key_table, mine, send(mine, by_core)),
        scalars=(0,),
        limit=16,
        scratch=[pltpu.VMEM((SPAN, query_width), BF16)],
    )

    sections = lax.axis_size("section")
    route = [(i, (i + 1) % sections) for i in range(sections)]
    rests, nears, first, second, layers, results = [], [], [], [], [], []

    def project_out(chunk, behind=()):
        keep, give = output_partial(attention, turned[chunk], behind)
        return CHUNKS[chunk], keep, give

    def round_1(width, keep, give, behind=()):
        to_up, to_down, rest = call(
            add_kernel,
            (shape(64, width), shape(64, width), shape(128, width, F32)),
            (keep, send(give, by_core)),
            behind=behind,
        )
        rests.append(rest)
        first.append((send(to_up, by_y(1)), send(to_down, by_y(-1))))

    def round_2(chunk, behind=()):
        width = CHUNKS[chunk]
        to_up, to_down, near = call(
            middle_kernel,
            (shape(64, width // 2), shape(64, width // 2), shape(64, width, F32)),
            (rests[chunk], *first[chunk]),
            behind=behind,
        )
        nears.append(near)
        second.append((send(to_up, by_y(1)), send(to_down, by_y(-1))))

    def round_3(chunk, behind=(), behind_last=()):
        width = CHUNKS[chunk]
        mine, to_z = call(
            last_kernel,
            (shape(32, width, F32), shape(32, width)),
            (nears[chunk], *second[chunk]),
            behind=behind,
        )
        layers.append(
            call(
                functools.partial(layer_kernel, starts[chunk]),
                shape(32, width),
                (mine, send(to_z, by_z), hidden, pair),
                behind=behind_last,
            )
        )
        results.append(lax.ppermute(layers[chunk], "section", route))

    parts = []
    for chunk in range(3):
        parts.append(project_out(chunk, (parts[-1][1],) if parts else ()))
    for chunk in range(3):
        round_1(*parts[chunk])
    round_2(0)
    round_3(0)
    round_2(1)
    round_3(1)
    round_2(2, (layers[0],))
    round_3(2, (layers[1],), (results[0],))
    return jnp.concatenate(results, axis=1)


def solution(mesh):
    placed = (
        P(("section", "tensor"), None),
        P("section", None),
        P("section", "tensor"),
        P("section", "tensor"),
        P(("section", "tensor"), None),
        P("section", "tensor"),
        P("section"),
    )
    return jax.shard_map(
        local, mesh=mesh, in_specs=placed, out_specs=P(("section", "tensor"), None), check_vma=False
    )
```

```python
import functools
import math

import jax
import jax.numpy as jnp
from jax import lax
from jax.experimental import pallas as pl
from jax.experimental.pallas import tpu as pltpu
from jax.sharding import PartitionSpec as P

HD = 128
HEADS = 32
KVH = 4
BLOCK = 128
GROUP = 16
ROWS = 32
SPAN = 512
CHUNKS = (2560, 3072, 2560)

NORM_EPS = 1e-05
SCALE_EPS = 1e-06
ROPE_BASE = 500000.0
F32 = jnp.float32
BF16 = jnp.bfloat16


def send(block, target):
    return lax.ppermute(block, "tensor", [(t, target(t)) for t in range(GROUP)])


def by_y(distance):
    return lambda t: (t & 9) | ((((t >> 1) + distance) & 3) << 1)


def by_z(t):
    return t ^ 8


def by_core(t):
    return t ^ 1


NEAR = [(0, 0), (0, 1), (0, 3), (1, 0)]
FAR = [(0, 2), (1, 1), (1, 3), (1, 2)]
ROWS_BY_ROWS = (((1,), (1,)), ((), ()))
NO_COST = pl.CostEstimate(flops=0, bytes_accessed=0, transcendentals=0)
VMEM = pl.BlockSpec(memory_space=pltpu.VMEM)
SMEM = pl.BlockSpec(memory_space=pltpu.SMEM)


def held_rows(position):
    z, y, core = position >> 3, (position >> 1) & 3, position & 1
    blocks = [
        ((z ^ dz) << 3) | (((y + dy) & 3) << 1) | (core ^ swap)
        for steps in (NEAR, FAR)
        for swap in (0, 1)
        for dz, dy in steps
    ]
    return (jnp.stack(blocks)[:, None] * ROWS + jnp.arange(ROWS, dtype=jnp.int32)).reshape(-1)


def hadamard(size):
    index = jnp.arange(size, dtype=jnp.int32)
    common = index[:, None] & index[None, :]
    parity = jnp.zeros((size, size), jnp.int32)
    for bit in range(size.bit_length() - 1):
        parity = parity + (common >> bit & 1)
    return jnp.where(parity % 2 == 0, 1.0, -1.0).astype(F32)


def call(kernel, shapes, inputs, scalars=(), behind=(), limit=12, scratch=()):
    count, waits = len(inputs), len(behind)
    specs = [SMEM if i in scalars else VMEM for i in range(count)]

    def body(*refs):
        kernel(*refs[:count], *refs[count + waits :])

    return pl.pallas_call(
        body,
        out_shape=shapes,
        in_specs=specs + [pl.BlockSpec(memory_space=pl.ANY)] * waits,
        out_specs=jax.tree.map(lambda _: VMEM, shapes),
        scratch_shapes=scratch,
        compiler_params=pltpu.CompilerParams(vmem_limit_bytes=limit << 20),
        cost_estimate=NO_COST,
    )(*inputs, *behind)


def shape(rows, columns, kind=BF16):
    return jax.ShapeDtypeStruct((rows, columns), kind)


def norm_kernel(x_ref, gain_ref, out_ref):
    values = x_ref[...].astype(F32)
    inverse = lax.rsqrt(jnp.mean(values * values, axis=1, keepdims=True) + NORM_EPS)
    out_ref[...] = (values * inverse * gain_ref[...]).astype(BF16)


def forward_kernel(own_ref, up_ref, down_ref, other_ref, to_down_ref, to_up_ref, to_z_ref, near_ref):
    full = own_ref.shape[1]
    half, quarter = full // 2, full // 4
    to_down_ref[:, :half] = up_ref[:, :half]
    to_down_ref[:, half:] = other_ref[:, :quarter]
    to_up_ref[:, :half] = down_ref[:, half:]
    to_up_ref[:, half:] = other_ref[:, :quarter]
    to_z_ref[:, : full - quarter] = up_ref[:, quarter:]
    to_z_ref[:, full - quarter :] = down_ref[:, quarter:]
    for place, ref in enumerate((own_ref, up_ref, down_ref, other_ref)):
        near_ref[place * ROWS : (place + 1) * ROWS, :] = ref[...]


def copy_kernel(in_ref, out_ref):
    out_ref[...] = in_ref[...]


def join_kernel(*refs):
    out_ref, at = refs[-1], 0
    for top, low in (refs[:2], refs[2:4]):
        rows, width = top.shape
        out_ref[:rows, at : at + width] = top[...]
        out_ref[rows:, at : at + width] = low[...]
        at += width


def near_kernel(step, mine_ref, theirs_ref, wq_ref, wkv_ref, q_ref, kv_ref):
    q = jnp.zeros(q_ref.shape, F32)
    kv = jnp.zeros(kv_ref.shape, F32)
    for start in range(0, wq_ref.shape[0], step):
        at = slice(start, start + step)
        rows = jnp.concatenate([mine_ref[:, at], theirs_ref[:, at]], axis=0)
        q += jnp.dot(rows, wq_ref[at, :], preferred_element_type=F32)
        kv += lax.dot_general(wkv_ref[:, at], rows, ROWS_BY_ROWS, preferred_element_type=F32)
    q_ref[...] = q
    kv_ref[...] = kv.astype(BF16)


def gathered(layout, pieces, start, step):
    parts = []
    for spans in layout:
        for which, low, high, base in spans:
            if low <= start < high:
                parts.append(pieces[which][:, base + start - low : base + start - low + step])
    return jnp.concatenate(parts, axis=0)


def far_keyval_kernel(layout, step, *refs):
    pieces, (wkv_ref, near_ref, order_ref, kv_ref) = refs[:-4], refs[-4:]
    kv = jnp.zeros(near_ref.shape, F32)
    for start in range(0, wkv_ref.shape[1], step):
        rows = gathered(layout, pieces, start, step)
        columns = wkv_ref[:, start : start + step]
        kv += lax.dot_general(columns, rows, ROWS_BY_ROWS, preferred_element_type=F32)
    both = jnp.concatenate([near_ref[...], kv.astype(BF16)], axis=1)
    kv_ref[...] = jnp.dot(both, order_ref[...], preferred_element_type=F32).astype(BF16)


def far_query_kernel(layout, step, *refs):
    pieces, (wq_ref, q_ref) = refs[:-2], refs[-2:]
    q = jnp.zeros(q_ref.shape, F32)
    for start in range(0, wq_ref.shape[0], step):
        rows = gathered(layout, pieces, start, step)
        q += jnp.dot(rows, wq_ref[start : start + step, :], preferred_element_type=F32)
    q_ref[...] = q


def pick(flags_ref, mine, theirs):
    half = mine.shape[0] // 2
    turned, core = flags_ref[0] != 0, flags_ref[1] != 0
    low = jnp.where(core, theirs, mine)
    high = jnp.where(core, mine, theirs)
    keys = jnp.concatenate(
        [jnp.where(turned, low[half:], low[:half]), jnp.where(turned, high[half:], high[:half])]
    )
    values = jnp.concatenate(
        [jnp.where(turned, low[:half], low[half:]), jnp.where(turned, high[:half], high[half:])]
    )
    return keys, values


TILE = 256


def attend_kernel(cached, flags_ref, qn_ref, qf_ref, row_ref, key_ref, mine_ref, theirs_ref, out_ref, joined_ref):
    keys, values = pick(flags_ref, mine_ref[...], theirs_ref[...])
    half = HD // 2
    first, second = keys[:half, cached:].astype(F32), keys[half:, cached:].astype(F32)
    cosine, sine = key_ref[:half, :], key_ref[half:, :]
    new_keys = jnp.concatenate(
        [first * cosine - second * sine, second * cosine + first * sine], axis=0
    ).astype(BF16)
    old_keys, old_values, new_values = keys[:, :cached], values[:, :cached], values[:, cached:]
    bias = jnp.where(
        lax.broadcasted_iota(jnp.int32, (1, cached), 1) < flags_ref[2], 0.0, -1e30
    )
    factor = 1.0 / math.sqrt(HD)
    for source, start in ((qn_ref, 0), (qf_ref, TILE)):
        at = slice(start, start + TILE)
        column = lax.broadcasted_iota(jnp.int32, (TILE, new_keys.shape[1]), 1)
        seen = column <= row_ref[at, 2 * HD : 2 * HD + 1].astype(jnp.int32)
        for head in range(2):
            columns = slice(head * HD, (head + 1) * HD)
            raw = source[:, columns]
            query = raw * row_ref[at, :HD] + pltpu.roll(raw, half, 1) * row_ref[at, HD : 2 * HD]
            query = query.astype(BF16)
            old = jnp.dot(query, old_keys, preferred_element_type=F32) * factor + bias
            new = jnp.dot(query, new_keys, preferred_element_type=F32) * factor
            new = jnp.where(seen, new, -1e30)
            top = jnp.maximum(
                jnp.max(old, axis=1, keepdims=True), jnp.max(new, axis=1, keepdims=True)
            )
            old, new = jnp.exp(old - top), jnp.exp(new - top)
            total = jnp.sum(old, axis=1, keepdims=True) + jnp.sum(new, axis=1, keepdims=True)
            value = lax.dot_general(
                old.astype(BF16), old_values, ROWS_BY_ROWS, preferred_element_type=F32
            )
            value += lax.dot_general(
                new.astype(BF16), new_values, ROWS_BY_ROWS, preferred_element_type=F32
            )
            joined_ref[at, columns] = (value / total).astype(BF16)
    for core in (0, 1):
        near, far = 4 * core, 8 + 4 * core
        order = (near, near + 3, near + 1, far + 1, near + 2, far + 2, far, far + 3)
        for place, block in enumerate(order):
            piece = joined_ref[block * ROWS : (block + 1) * ROWS, :]
            to = slice((8 * core + place) * ROWS, (8 * core + place + 1) * ROWS)
            out_ref[to, : 2 * HD] = piece
            out_ref[to, 2 * HD :] = piece


def turn_kernel(w_ref, table_ref, out_ref):
    rows = w_ref.shape[0]
    for start in range(0, w_ref.shape[1], 2 * BLOCK):
        at = slice(start, start + 2 * BLOCK)
        turned = jnp.dot(w_ref[:, at], table_ref[...], preferred_element_type=F32)
        turned = turned * (1.0 / math.sqrt(BLOCK))
        high = turned.astype(BF16)
        out_ref[:rows, at] = high
        out_ref[rows:, at] = (turned - high.astype(F32)).astype(BF16)


def turn_weights(w_out, table, start, width, behind, tile=512):
    rows = w_out.shape[0]
    return pl.pallas_call(
        lambda w_ref, table_ref, behind_ref, out_ref: turn_kernel(w_ref, table_ref, out_ref),
        grid=(width // tile,),
        in_specs=[
            pl.BlockSpec((rows, tile), lambda i: (0, start // tile + i)),
            pl.BlockSpec(table.shape, lambda i: (0, 0)),
            pl.BlockSpec(memory_space=pl.ANY),
        ],
        out_specs=pl.BlockSpec((2 * rows, tile), lambda i: (0, i)),
        out_shape=jax.ShapeDtypeStruct((2 * rows, width), BF16),
        compiler_params=pltpu.CompilerParams(vmem_limit_bytes=8 << 20),
        cost_estimate=NO_COST,
    )(w_out, table, behind)


def output_kernel(att_ref, w_ref, keep_ref, give_ref):
    half = keep_ref.shape[0]
    for start in range(0, w_ref.shape[1], 2 * BLOCK):
        pair = jnp.dot(
            att_ref[...], w_ref[:, start : start + 2 * BLOCK], preferred_element_type=F32
        )
        for at in range(0, 2 * BLOCK, BLOCK):
            block = pair[:, at : at + BLOCK]
            scale = jnp.max(jnp.abs(block), axis=1, keepdims=True) + SCALE_EPS
            level = (block * (1.0 / scale)).astype(BF16)
            value = (scale * level.astype(F32)).astype(BF16)
            columns = slice(start + at, start + at + BLOCK)
            keep_ref[:, columns] = value[:half]
            give_ref[:, columns] = value[half:]


def output_partial(attention, turned, behind=(), tile=512):
    rows, depth = attention.shape
    width = turned.shape[1]
    half, waits = shape(rows // 2, width), len(behind)
    return pl.pallas_call(
        lambda *refs: output_kernel(*refs[:2], *refs[2 + waits :]),
        grid=(width // tile,),
        in_specs=[
            pl.BlockSpec((rows, depth), lambda i: (0, 0)),
            pl.BlockSpec((depth, tile), lambda i: (0, i)),
        ]
        + [pl.BlockSpec(memory_space=pl.ANY)] * waits,
        out_specs=(
            pl.BlockSpec((rows // 2, tile), lambda i: (0, i)),
            pl.BlockSpec((rows // 2, tile), lambda i: (0, i)),
        ),
        out_shape=(half, half),
        compiler_params=pltpu.CompilerParams(vmem_limit_bytes=10 << 20),
        cost_estimate=pl.CostEstimate(
            flops=5000000 * width, bytes_accessed=0, transcendentals=0
        ),
    )(attention, turned, *behind)


def gather_head(block):
    got = []
    for turn in range(2):
        pairs = []
        for t in range(GROUP):
            head, chip, core = t >> 2, (t >> 1) & 1, t & 1
            pairs.append((8 * (chip ^ turn) + 2 * head + core, t))
        got.append(lax.ppermute(block, "tensor", pairs))
    return got


def add_kernel(keep_ref, got_ref, to_up_ref, to_down_ref, rest_ref):
    half = to_up_ref.shape[1] // 2
    left, right = slice(0, half), slice(half, 2 * half)

    def total(first, last, columns):
        return keep_ref[first:last, columns].astype(F32) + got_ref[first:last, columns].astype(F32)

    to_up_ref[:, left] = total(192, 256, left).astype(BF16)
    to_up_ref[:, right] = total(64, 128, right).astype(BF16)
    to_down_ref[:, left] = total(128, 192, left).astype(BF16)
    to_down_ref[:, right] = total(192, 256, right).astype(BF16)
    rest_ref[:64, left] = total(0, 64, left)
    rest_ref[:64, right] = total(0, 64, right)
    rest_ref[64:, left] = total(64, 128, left)
    rest_ref[64:, right] = total(128, 192, right)


def middle_kernel(rest_ref, from_down_ref, from_up_ref, to_up_ref, to_down_ref, near_ref):
    half = to_up_ref.shape[1]
    left, right = slice(0, half), slice(half, 2 * half)
    to_up_ref[...] = (rest_ref[64:, left] + from_down_ref[:, left].astype(F32)).astype(BF16)
    to_down_ref[...] = (rest_ref[64:, right] + from_up_ref[:, right].astype(F32)).astype(BF16)
    near_ref[:, left] = rest_ref[:64, left] + from_up_ref[:, left].astype(F32)
    near_ref[:, right] = rest_ref[:64, right] + from_down_ref[:, right].astype(F32)


def last_kernel(near_ref, from_down_ref, from_up_ref, mine_ref, to_z_ref):
    half = from_up_ref.shape[1]
    for at, ref in ((0, from_down_ref), (half, from_up_ref)):
        columns = slice(at, at + half)
        total = near_ref[:, columns] + ref[...].astype(F32)
        mine_ref[:, columns] = total[:32]
        to_z_ref[:, columns] = total[32:].astype(BF16)


def select_kernel(flags_ref, first_ref, second_ref, out_ref):
    out_ref[...] = jnp.where(flags_ref[3] != 0, first_ref[...], second_ref[...])


def layer_kernel(start, mine_ref, from_z_ref, hidden_ref, table_ref, out_ref):
    total = mine_ref[...] + from_z_ref[...].astype(F32)
    for at in range(0, total.shape[1], 2 * BLOCK):
        rest = total[:, at : at + 2 * BLOCK]
        restored = jnp.zeros(rest.shape, F32)
        for _ in range(3):
            part = rest.astype(BF16)
            restored += jnp.dot(part, table_ref[...], preferred_element_type=F32)
            rest = rest - part.astype(F32)
        before = hidden_ref[:, start + at : start + at + 2 * BLOCK].astype(F32)
        out_ref[:, at : at + 2 * BLOCK] = (before + restored * (1.0 / math.sqrt(BLOCK))).astype(BF16)


def local(hidden, gain, w_query, w_keyval, w_out, cache_kv, offsets):
    position = lax.axis_index("tensor")
    offset = offsets[0]
    full = w_query.shape[0]
    normed = call(norm_kernel, shape(*hidden.shape), (hidden, gain))

    up = send(normed, by_y(-1))
    down = send(normed, by_y(1))
    other = send(normed, by_z)

    held = held_rows(position)
    span = jnp.arange(SPAN, dtype=jnp.int32)
    order = (held[:, None] == span[None, :]).astype(BF16)
    freqs = ROPE_BASE ** (-(2.0 / HD) * jnp.arange(HD // 2, dtype=F32))
    angles = (offset + held).astype(F32)[:, None] * freqs[None, :]
    cosine, sine = jnp.cos(angles), jnp.sin(angles)
    index = jnp.broadcast_to(held.astype(F32)[:, None], (SPAN, HD))
    row_table = jnp.concatenate([cosine, cosine, -sine, sine, index], axis=1)
    angles = freqs[:, None] * (offset + span).astype(F32)[None, :]
    key_table = jnp.concatenate([jnp.cos(angles), jnp.sin(angles)], axis=0)
    section = lax.axis_index("section")
    edge = (section & 3) == 0
    flags = jnp.stack([(position >> 1) & 1, position & 1, offset, edge]).astype(jnp.int32)
    table = hadamard(BLOCK)
    zero = jnp.zeros_like(table)
    pair = jnp.concatenate(
        [jnp.concatenate([table, zero], axis=1), jnp.concatenate([zero, table], axis=1)], axis=0
    ).astype(BF16)
    starts = [sum(CHUNKS[:i]) for i in range(len(CHUNKS))]

    half, quarter = full // 2, full // 4
    to_down, to_up, to_z, near = call(
        forward_kernel,
        (shape(ROWS, half + quarter), shape(ROWS, half + quarter), shape(ROWS, 2 * (full - quarter)), shape(4 * ROWS, full)),
        (normed, up, down, other),
        behind=(order, row_table, key_table, pair),
    )
    from_up = send(to_down, by_y(-1))
    from_down = send(to_up, by_y(1))
    from_z = send(to_z, by_z)
    far = send(other, by_y(2))
    near_theirs = send(near, by_core)
    turned = [turn_weights(w_out, pair, at, width, to_z) for at, width in zip(starts, CHUNKS)]
    layout = []
    for base in (0, 4):
        layout += [
            [(base, 0, half, 0), (base + 1, half, full, 0)],
            [(base, 0, quarter, half), (base + 2, quarter, full, 0)],
            [(base + 1, 0, quarter, half), (base + 2, quarter, full, full - quarter)],
            [(base + 3, 0, full, 0)],
        ]
    query_width, kv_width = w_query.shape[1], w_keyval.shape[1]
    rows, cached = SPAN // 2, cache_kv.shape[0]
    q_near, kv_near = call(
        functools.partial(near_kernel, 1024),
        (shape(rows, query_width, F32), shape(kv_width, rows)),
        (near, near_theirs, w_query, w_keyval.T),
        behind=turned,
    )
    distant = [from_up, from_down, from_z, far]
    cache = call(copy_kernel, shape(kv_width, cached), (cache_kv.T,), behind=distant)
    from_z = call(copy_kernel, shape(*from_z.shape), (from_z,), behind=(kv_near,))
    distant = distant + [send(piece, by_core) for piece in (from_up, from_down, from_z, far)]
    cache = gather_head(cache)
    keyval = call(
        functools.partial(far_keyval_kernel, layout, 1024),
        shape(kv_width, SPAN),
        (*distant, w_keyval.T, kv_near, order),
    )
    new = gather_head(keyval)
    q_far = call(
        functools.partial(far_query_kernel, layout, 1024),
        shape(rows, query_width, F32),
        (*distant, w_query),
        behind=(keyval,),
    )
    mine = call(join_kernel, shape(2 * kv_width, cached + SPAN), (*cache, *new), behind=(q_far,))
    attention = call(
        functools.partial(attend_kernel, cached),
        shape(SPAN, 2 * query_width),
        (flags, q_near, q_far, row_table, key_table, mine, send(mine, by_core)),
        scalars=(0,),
        limit=16,
        scratch=[pltpu.VMEM((SPAN, query_width), BF16)],
    )

    sections = lax.axis_size("section")
    route = [(i, (i + 1) % sections) for i in range(sections)]
    along_x = [(i, (i & ~3) | ((i + 1) & 3)) for i in range(sections)]
    along_z = [(i, (i + 4) % sections) for i in range(0, sections, 4)]

    def hand_on(block, around=None):
        if around is None:
            return lax.ppermute(block, "section", route)
        beside = lax.ppermute(block, "section", along_x)
        above = lax.ppermute(beside, "section", along_z)
        return call(
            select_kernel, shape(*block.shape), (flags, above, beside), scalars=(0,), behind=around
        )

    rests, nears, first, second, layers, results = [], [], [], [], [], []

    def project_out(chunk, behind=()):
        keep, give = output_partial(attention, turned[chunk], behind)
        return CHUNKS[chunk], keep, give

    def round_1(width, keep, give, behind=()):
        to_up, to_down, rest = call(
            add_kernel,
            (shape(64, width), shape(64, width), shape(128, width, F32)),
            (keep, send(give, by_core)),
            behind=behind,
        )
        rests.append(rest)
        first.append((send(to_up, by_y(1)), send(to_down, by_y(-1))))

    def round_2(chunk, behind=()):
        width = CHUNKS[chunk]
        to_up, to_down, near = call(
            middle_kernel,
            (shape(64, width // 2), shape(64, width // 2), shape(64, width, F32)),
            (rests[chunk], *first[chunk]),
            behind=behind,
        )
        nears.append(near)
        second.append((send(to_up, by_y(1)), send(to_down, by_y(-1))))

    def round_3(chunk, behind=(), behind_last=()):
        width = CHUNKS[chunk]
        mine, to_z = call(
            last_kernel,
            (shape(32, width, F32), shape(32, width)),
            (nears[chunk], *second[chunk]),
            behind=behind,
        )
        layers.append(
            call(
                functools.partial(layer_kernel, starts[chunk]),
                shape(32, width),
                (mine, send(to_z, by_z), hidden, pair),
                behind=behind_last,
            )
        )
        results.append(hand_on(layers[chunk], () if chunk == 1 else None))

    parts = []
    for chunk in range(3):
        parts.append(project_out(chunk, (parts[-1][1],) if parts else ()))
    for chunk in range(3):
        round_1(*parts[chunk])
    round_2(0)
    round_3(0)
    round_2(1)
    round_3(1)
    round_2(2, (layers[0],))
    round_3(2, (layers[1],), (results[0],))
    return jnp.concatenate(results, axis=1)


def solution(mesh):
    placed = (
        P(("section", "tensor"), None),
        P("section", None),
        P("section", "tensor"),
        P("section", "tensor"),
        P(("section", "tensor"), None),
        P("section", "tensor"),
        P("section"),
    )
    return jax.shard_map(
        local, mesh=mesh, in_specs=placed, out_specs=P(("section", "tensor"), None), check_vma=False
    )
```

```python
import functools
import math

import jax
import jax.numpy as jnp
from jax import lax
from jax.experimental import pallas as pl
from jax.experimental.pallas import tpu as pltpu
from jax.sharding import PartitionSpec as P

HD = 128
HEADS = 32
KVH = 4
BLOCK = 128
GROUP = 16
ROWS = 32
SPAN = 512
CHUNKS = (3072, 3072, 2048)

NORM_EPS = 1e-05
SCALE_EPS = 1e-06
ROPE_BASE = 500000.0
F32 = jnp.float32
BF16 = jnp.bfloat16


def send(block, target):
    return lax.ppermute(block, "tensor", [(t, target(t)) for t in range(GROUP)])


def by_y(distance):
    return lambda t: (t & 9) | ((((t >> 1) + distance) & 3) << 1)


def by_z(t):
    return t ^ 8


def by_core(t):
    return t ^ 1


NEAR = [(0, 0), (0, 1), (0, 3), (1, 0)]
FAR = [(0, 2), (1, 1), (1, 3), (1, 2)]
ROWS_BY_ROWS = (((1,), (1,)), ((), ()))
NO_COST = pl.CostEstimate(flops=0, bytes_accessed=0, transcendentals=0)
VMEM = pl.BlockSpec(memory_space=pltpu.VMEM)
SMEM = pl.BlockSpec(memory_space=pltpu.SMEM)


def held_rows(position):
    z, y, core = position >> 3, (position >> 1) & 3, position & 1
    blocks = [
        ((z ^ dz) << 3) | (((y + dy) & 3) << 1) | (core ^ swap)
        for steps in (NEAR, FAR)
        for swap in (0, 1)
        for dz, dy in steps
    ]
    return (jnp.stack(blocks)[:, None] * ROWS + jnp.arange(ROWS, dtype=jnp.int32)).reshape(-1)


def hadamard(size):
    index = jnp.arange(size, dtype=jnp.int32)
    common = index[:, None] & index[None, :]
    parity = jnp.zeros((size, size), jnp.int32)
    for bit in range(size.bit_length() - 1):
        parity = parity + (common >> bit & 1)
    return jnp.where(parity % 2 == 0, 1.0, -1.0).astype(F32)


def call(kernel, shapes, inputs, scalars=(), behind=(), limit=12, scratch=()):
    count, waits = len(inputs), len(behind)
    specs = [SMEM if i in scalars else VMEM for i in range(count)]

    def body(*refs):
        kernel(*refs[:count], *refs[count + waits :])

    return pl.pallas_call(
        body,
        out_shape=shapes,
        in_specs=specs + [pl.BlockSpec(memory_space=pl.ANY)] * waits,
        out_specs=jax.tree.map(lambda _: VMEM, shapes),
        scratch_shapes=scratch,
        compiler_params=pltpu.CompilerParams(vmem_limit_bytes=limit << 20),
        cost_estimate=NO_COST,
    )(*inputs, *behind)


def shape(rows, columns, kind=BF16):
    return jax.ShapeDtypeStruct((rows, columns), kind)


def norm_kernel(x_ref, gain_ref, out_ref):
    values = x_ref[...].astype(F32)
    inverse = lax.rsqrt(jnp.mean(values * values, axis=1, keepdims=True) + NORM_EPS)
    out_ref[...] = (values * inverse * gain_ref[...]).astype(BF16)


def forward_kernel(own_ref, up_ref, down_ref, other_ref, to_down_ref, to_up_ref, to_z_ref, near_ref):
    full = own_ref.shape[1]
    half, quarter = full // 2, full // 4
    to_down_ref[:, :half] = up_ref[:, :half]
    to_down_ref[:, half:] = other_ref[:, :quarter]
    to_up_ref[:, :half] = down_ref[:, half:]
    to_up_ref[:, half:] = other_ref[:, :quarter]
    to_z_ref[:, : full - quarter] = up_ref[:, quarter:]
    to_z_ref[:, full - quarter :] = down_ref[:, quarter:]
    for place, ref in enumerate((own_ref, up_ref, down_ref, other_ref)):
        near_ref[place * ROWS : (place + 1) * ROWS, :] = ref[...]


def copy_kernel(in_ref, out_ref):
    out_ref[...] = in_ref[...]


def join_kernel(*refs):
    out_ref, at = refs[-1], 0
    for top, low in (refs[:2], refs[2:4]):
        rows, width = top.shape
        out_ref[:rows, at : at + width] = top[...]
        out_ref[rows:, at : at + width] = low[...]
        at += width


def near_kernel(step, mine_ref, theirs_ref, wq_ref, wkv_ref, q_ref, kv_ref):
    q = jnp.zeros(q_ref.shape, F32)
    kv = jnp.zeros(kv_ref.shape, F32)
    for start in range(0, wq_ref.shape[0], step):
        at = slice(start, start + step)
        rows = jnp.concatenate([mine_ref[:, at], theirs_ref[:, at]], axis=0)
        q += jnp.dot(rows, wq_ref[at, :], preferred_element_type=F32)
        kv += lax.dot_general(wkv_ref[:, at], rows, ROWS_BY_ROWS, preferred_element_type=F32)
    q_ref[...] = q
    kv_ref[...] = kv.astype(BF16)


def gathered(layout, pieces, start, step):
    parts = []
    for spans in layout:
        for which, low, high, base in spans:
            if low <= start < high:
                parts.append(pieces[which][:, base + start - low : base + start - low + step])
    return jnp.concatenate(parts, axis=0)


def far_keyval_kernel(layout, step, *refs):
    pieces, (wkv_ref, near_ref, order_ref, kv_ref) = refs[:-4], refs[-4:]
    kv = jnp.zeros(near_ref.shape, F32)
    for start in range(0, wkv_ref.shape[1], step):
        rows = gathered(layout, pieces, start, step)
        columns = wkv_ref[:, start : start + step]
        kv += lax.dot_general(columns, rows, ROWS_BY_ROWS, preferred_element_type=F32)
    both = jnp.concatenate([near_ref[...], kv.astype(BF16)], axis=1)
    kv_ref[...] = jnp.dot(both, order_ref[...], preferred_element_type=F32).astype(BF16)


def far_query_kernel(layout, step, *refs):
    pieces, (wq_ref, q_ref) = refs[:-2], refs[-2:]
    q = jnp.zeros(q_ref.shape, F32)
    for start in range(0, wq_ref.shape[0], step):
        rows = gathered(layout, pieces, start, step)
        q += jnp.dot(rows, wq_ref[start : start + step, :], preferred_element_type=F32)
    q_ref[...] = q


def pick(flags_ref, mine, theirs):
    half = mine.shape[0] // 2
    turned, core = flags_ref[0] != 0, flags_ref[1] != 0
    low = jnp.where(core, theirs, mine)
    high = jnp.where(core, mine, theirs)
    keys = jnp.concatenate(
        [jnp.where(turned, low[half:], low[:half]), jnp.where(turned, high[half:], high[:half])]
    )
    values = jnp.concatenate(
        [jnp.where(turned, low[:half], low[half:]), jnp.where(turned, high[:half], high[half:])]
    )
    return keys, values


TILE = 256


def attend_kernel(cached, flags_ref, qn_ref, qf_ref, row_ref, key_ref, mine_ref, theirs_ref, out_ref, joined_ref):
    keys, values = pick(flags_ref, mine_ref[...], theirs_ref[...])
    half = HD // 2
    first, second = keys[:half, cached:].astype(F32), keys[half:, cached:].astype(F32)
    cosine, sine = key_ref[:half, :], key_ref[half:, :]
    new_keys = jnp.concatenate(
        [first * cosine - second * sine, second * cosine + first * sine], axis=0
    ).astype(BF16)
    old_keys, old_values, new_values = keys[:, :cached], values[:, :cached], values[:, cached:]
    bias = jnp.where(
        lax.broadcasted_iota(jnp.int32, (1, cached), 1) < flags_ref[2], 0.0, -1e30
    )
    factor = 1.0 / math.sqrt(HD)
    for source, start in ((qn_ref, 0), (qf_ref, TILE)):
        at = slice(start, start + TILE)
        column = lax.broadcasted_iota(jnp.int32, (TILE, new_keys.shape[1]), 1)
        seen = column <= row_ref[at, 2 * HD : 2 * HD + 1].astype(jnp.int32)
        for head in range(2):
            columns = slice(head * HD, (head + 1) * HD)
            raw = source[:, columns]
            query = raw * row_ref[at, :HD] + pltpu.roll(raw, half, 1) * row_ref[at, HD : 2 * HD]
            query = query.astype(BF16)
            old = jnp.dot(query, old_keys, preferred_element_type=F32) * factor + bias
            new = jnp.dot(query, new_keys, preferred_element_type=F32) * factor
            new = jnp.where(seen, new, -1e30)
            top = jnp.maximum(
                jnp.max(old, axis=1, keepdims=True), jnp.max(new, axis=1, keepdims=True)
            )
            old, new = jnp.exp(old - top), jnp.exp(new - top)
            total = jnp.sum(old, axis=1, keepdims=True) + jnp.sum(new, axis=1, keepdims=True)
            value = lax.dot_general(
                old.astype(BF16), old_values, ROWS_BY_ROWS, preferred_element_type=F32
            )
            value += lax.dot_general(
                new.astype(BF16), new_values, ROWS_BY_ROWS, preferred_element_type=F32
            )
            joined_ref[at, columns] = (value / total).astype(BF16)
    for core in (0, 1):
        near, far = 4 * core, 8 + 4 * core
        order = (near, near + 3, near + 1, far + 1, near + 2, far + 2, far, far + 3)
        for place, block in enumerate(order):
            piece = joined_ref[block * ROWS : (block + 1) * ROWS, :]
            to = slice((8 * core + place) * ROWS, (8 * core + place + 1) * ROWS)
            out_ref[to, : 2 * HD] = piece
            out_ref[to, 2 * HD :] = piece


def turn_kernel(w_ref, table_ref, out_ref):
    rows = w_ref.shape[0]
    for start in range(0, w_ref.shape[1], 2 * BLOCK):
        at = slice(start, start + 2 * BLOCK)
        turned = jnp.dot(w_ref[:, at], table_ref[...], preferred_element_type=F32)
        turned = turned * (1.0 / math.sqrt(BLOCK))
        high = turned.astype(BF16)
        out_ref[:rows, at] = high
        out_ref[rows:, at] = (turned - high.astype(F32)).astype(BF16)


def turn_weights(w_out, table, start, width, behind, tile=512):
    rows = w_out.shape[0]
    return pl.pallas_call(
        lambda w_ref, table_ref, behind_ref, out_ref: turn_kernel(w_ref, table_ref, out_ref),
        grid=(width // tile,),
        in_specs=[
            pl.BlockSpec((rows, tile), lambda i: (0, start // tile + i)),
            pl.BlockSpec(table.shape, lambda i: (0, 0)),
            pl.BlockSpec(memory_space=pl.ANY),
        ],
        out_specs=pl.BlockSpec((2 * rows, tile), lambda i: (0, i)),
        out_shape=jax.ShapeDtypeStruct((2 * rows, width), BF16),
        compiler_params=pltpu.CompilerParams(vmem_limit_bytes=8 << 20),
        cost_estimate=NO_COST,
    )(w_out, table, behind)


def output_kernel(att_ref, w_ref, keep_ref, give_ref):
    half = keep_ref.shape[0]
    for start in range(0, w_ref.shape[1], 2 * BLOCK):
        pair = jnp.dot(
            att_ref[...], w_ref[:, start : start + 2 * BLOCK], preferred_element_type=F32
        )
        for at in range(0, 2 * BLOCK, BLOCK):
            block = pair[:, at : at + BLOCK]
            scale = jnp.max(jnp.abs(block), axis=1, keepdims=True) + SCALE_EPS
            level = (block * (1.0 / scale)).astype(BF16)
            value = (scale * level.astype(F32)).astype(BF16)
            columns = slice(start + at, start + at + BLOCK)
            keep_ref[:, columns] = value[:half]
            give_ref[:, columns] = value[half:]


def output_partial(attention, turned, behind=(), tile=512):
    rows, depth = attention.shape
    width = turned.shape[1]
    half, waits = shape(rows // 2, width), len(behind)
    return pl.pallas_call(
        lambda *refs: output_kernel(*refs[:2], *refs[2 + waits :]),
        grid=(width // tile,),
        in_specs=[
            pl.BlockSpec((rows, depth), lambda i: (0, 0)),
            pl.BlockSpec((depth, tile), lambda i: (0, i)),
        ]
        + [pl.BlockSpec(memory_space=pl.ANY)] * waits,
        out_specs=(
            pl.BlockSpec((rows // 2, tile), lambda i: (0, i)),
            pl.BlockSpec((rows // 2, tile), lambda i: (0, i)),
        ),
        out_shape=(half, half),
        compiler_params=pltpu.CompilerParams(vmem_limit_bytes=10 << 20),
        cost_estimate=pl.CostEstimate(
            flops=5000000 * width, bytes_accessed=0, transcendentals=0
        ),
    )(attention, turned, *behind)


def gather_head(block):
    got = []
    for turn in range(2):
        pairs = []
        for t in range(GROUP):
            head, chip, core = t >> 2, (t >> 1) & 1, t & 1
            pairs.append((8 * (chip ^ turn) + 2 * head + core, t))
        got.append(lax.ppermute(block, "tensor", pairs))
    return got


def add_kernel(keep_ref, got_ref, to_up_ref, to_down_ref, rest_ref):
    half = to_up_ref.shape[1] // 2
    left, right = slice(0, half), slice(half, 2 * half)

    def total(first, last, columns):
        return keep_ref[first:last, columns].astype(F32) + got_ref[first:last, columns].astype(F32)

    to_up_ref[:, left] = total(192, 256, left).astype(BF16)
    to_up_ref[:, right] = total(64, 128, right).astype(BF16)
    to_down_ref[:, left] = total(128, 192, left).astype(BF16)
    to_down_ref[:, right] = total(192, 256, right).astype(BF16)
    rest_ref[:64, left] = total(0, 64, left)
    rest_ref[:64, right] = total(0, 64, right)
    rest_ref[64:, left] = total(64, 128, left)
    rest_ref[64:, right] = total(128, 192, right)


def middle_kernel(rest_ref, from_down_ref, from_up_ref, to_up_ref, to_down_ref, near_ref):
    half = to_up_ref.shape[1]
    left, right = slice(0, half), slice(half, 2 * half)
    to_up_ref[...] = (rest_ref[64:, left] + from_down_ref[:, left].astype(F32)).astype(BF16)
    to_down_ref[...] = (rest_ref[64:, right] + from_up_ref[:, right].astype(F32)).astype(BF16)
    near_ref[:, left] = rest_ref[:64, left] + from_up_ref[:, left].astype(F32)
    near_ref[:, right] = rest_ref[:64, right] + from_down_ref[:, right].astype(F32)


def last_kernel(near_ref, from_down_ref, from_up_ref, mine_ref, to_z_ref):
    half = from_up_ref.shape[1]
    for at, ref in ((0, from_down_ref), (half, from_up_ref)):
        columns = slice(at, at + half)
        total = near_ref[:, columns] + ref[...].astype(F32)
        mine_ref[:, columns] = total[:32]
        to_z_ref[:, columns] = total[32:].astype(BF16)


def select_kernel(flags_ref, first_ref, second_ref, out_ref):
    out_ref[...] = jnp.where(flags_ref[3] != 0, first_ref[...], second_ref[...])


def layer_kernel(start, mine_ref, from_z_ref, hidden_ref, table_ref, out_ref):
    total = mine_ref[...] + from_z_ref[...].astype(F32)
    for at in range(0, total.shape[1], 2 * BLOCK):
        rest = total[:, at : at + 2 * BLOCK]
        restored = jnp.zeros(rest.shape, F32)
        for _ in range(3):
            part = rest.astype(BF16)
            restored += jnp.dot(part, table_ref[...], preferred_element_type=F32)
            rest = rest - part.astype(F32)
        before = hidden_ref[:, start + at : start + at + 2 * BLOCK].astype(F32)
        out_ref[:, at : at + 2 * BLOCK] = (before + restored * (1.0 / math.sqrt(BLOCK))).astype(BF16)


def local(hidden, gain, w_query, w_keyval, w_out, cache_kv, offsets):
    position = lax.axis_index("tensor")
    offset = offsets[0]
    full = w_query.shape[0]
    normed = call(norm_kernel, shape(*hidden.shape), (hidden, gain))

    up = send(normed, by_y(-1))
    down = send(normed, by_y(1))
    other = send(normed, by_z)

    held = held_rows(position)
    span = jnp.arange(SPAN, dtype=jnp.int32)
    order = (held[:, None] == span[None, :]).astype(BF16)
    freqs = ROPE_BASE ** (-(2.0 / HD) * jnp.arange(HD // 2, dtype=F32))
    angles = (offset + held).astype(F32)[:, None] * freqs[None, :]
    cosine, sine = jnp.cos(angles), jnp.sin(angles)
    index = jnp.broadcast_to(held.astype(F32)[:, None], (SPAN, HD))
    row_table = jnp.concatenate([cosine, cosine, -sine, sine, index], axis=1)
    angles = freqs[:, None] * (offset + span).astype(F32)[None, :]
    key_table = jnp.concatenate([jnp.cos(angles), jnp.sin(angles)], axis=0)
    section = lax.axis_index("section")
    edge = (section & 3) == 0
    flags = jnp.stack([(position >> 1) & 1, position & 1, offset, edge]).astype(jnp.int32)
    table = hadamard(BLOCK)
    zero = jnp.zeros_like(table)
    pair = jnp.concatenate(
        [jnp.concatenate([table, zero], axis=1), jnp.concatenate([zero, table], axis=1)], axis=0
    ).astype(BF16)
    starts = [sum(CHUNKS[:i]) for i in range(len(CHUNKS))]

    half, quarter = full // 2, full // 4
    to_down, to_up, to_z, near = call(
        forward_kernel,
        (shape(ROWS, half + quarter), shape(ROWS, half + quarter), shape(ROWS, 2 * (full - quarter)), shape(4 * ROWS, full)),
        (normed, up, down, other),
        behind=(order, row_table, key_table, pair),
    )
    from_up = send(to_down, by_y(-1))
    from_down = send(to_up, by_y(1))
    from_z = send(to_z, by_z)
    far = send(other, by_y(2))
    near_theirs = send(near, by_core)
    turned = [turn_weights(w_out, pair, at, width, to_z) for at, width in zip(starts, CHUNKS)]
    layout = []
    for base in (0, 4):
        layout += [
            [(base, 0, half, 0), (base + 1, half, full, 0)],
            [(base, 0, quarter, half), (base + 2, quarter, full, 0)],
            [(base + 1, 0, quarter, half), (base + 2, quarter, full, full - quarter)],
            [(base + 3, 0, full, 0)],
        ]
    query_width, kv_width = w_query.shape[1], w_keyval.shape[1]
    rows, cached = SPAN // 2, cache_kv.shape[0]
    q_near, kv_near = call(
        functools.partial(near_kernel, 1024),
        (shape(rows, query_width, F32), shape(kv_width, rows)),
        (near, near_theirs, w_query, w_keyval.T),
        behind=turned,
    )
    distant = [from_up, from_down, from_z, far]
    cache = call(copy_kernel, shape(kv_width, cached), (cache_kv.T,), behind=distant)
    from_z = call(copy_kernel, shape(*from_z.shape), (from_z,), behind=(kv_near,))
    distant = distant + [send(piece, by_core) for piece in (from_up, from_down, from_z, far)]
    cache = gather_head(cache)
    keyval = call(
        functools.partial(far_keyval_kernel, layout, 1024),
        shape(kv_width, SPAN),
        (*distant, w_keyval.T, kv_near, order),
    )
    new = gather_head(keyval)
    q_far = call(
        functools.partial(far_query_kernel, layout, 1024),
        shape(rows, query_width, F32),
        (*distant, w_query),
        behind=(keyval,),
    )
    mine = call(join_kernel, shape(2 * kv_width, cached + SPAN), (*cache, *new), behind=(q_far,))
    attention = call(
        functools.partial(attend_kernel, cached),
        shape(SPAN, 2 * query_width),
        (flags, q_near, q_far, row_table, key_table, mine, send(mine, by_core)),
        scalars=(0,),
        limit=16,
        scratch=[pltpu.VMEM((SPAN, query_width), BF16)],
    )

    sections = lax.axis_size("section")
    route = [(i, (i + 1) % sections) for i in range(sections)]
    along_x = [(i, (i & ~3) | ((i + 1) & 3)) for i in range(sections)]
    along_z = [(i, (i + 4) % sections) for i in range(0, sections, 4)]

    def hand_on(block, around=None):
        if around is None:
            return lax.ppermute(block, "section", route)
        beside = lax.ppermute(block, "section", along_x)
        above = lax.ppermute(beside, "section", along_z)
        return call(
            select_kernel, shape(*block.shape), (flags, above, beside), scalars=(0,), behind=around
        )

    rests, nears, first, second, layers, results = [], [], [], [], [], []

    def project_out(chunk, behind=()):
        keep, give = output_partial(attention, turned[chunk], behind)
        return CHUNKS[chunk], keep, give

    def round_1(width, keep, give, behind=()):
        to_up, to_down, rest = call(
            add_kernel,
            (shape(64, width), shape(64, width), shape(128, width, F32)),
            (keep, send(give, by_core)),
            behind=behind,
        )
        rests.append(rest)
        first.append((send(to_up, by_y(1)), send(to_down, by_y(-1))))

    def round_2(chunk, behind=()):
        width = CHUNKS[chunk]
        to_up, to_down, near = call(
            middle_kernel,
            (shape(64, width // 2), shape(64, width // 2), shape(64, width, F32)),
            (rests[chunk], *first[chunk]),
            behind=behind,
        )
        nears.append(near)
        second.append((send(to_up, by_y(1)), send(to_down, by_y(-1))))

    def round_3(chunk, behind=(), behind_last=()):
        width = CHUNKS[chunk]
        mine, to_z = call(
            last_kernel,
            (shape(32, width, F32), shape(32, width)),
            (nears[chunk], *second[chunk]),
            behind=behind,
        )
        layers.append(
            call(
                functools.partial(layer_kernel, starts[chunk]),
                shape(32, width),
                (mine, send(to_z, by_z), hidden, pair),
                behind=behind_last,
            )
        )
        results.append(hand_on(layers[chunk], () if chunk == 1 else None))

    parts = []
    for chunk in range(3):
        parts.append(project_out(chunk, (parts[-1][1],) if parts else ()))
    for chunk in range(3):
        round_1(*parts[chunk])
    round_2(0)
    round_3(0)
    round_2(1)
    round_3(1)
    round_2(2, (layers[0],))
    round_3(2, (layers[1],), (results[0],))
    return jnp.concatenate(results, axis=1)


def solution(mesh):
    placed = (
        P(("section", "tensor"), None),
        P("section", None),
        P("section", "tensor"),
        P("section", "tensor"),
        P(("section", "tensor"), None),
        P("section", "tensor"),
        P("section"),
    )
    return jax.shard_map(
        local, mesh=mesh, in_specs=placed, out_specs=P(("section", "tensor"), None), check_vma=False
    )
```

```python
import functools
import math

import jax
import jax.numpy as jnp
from jax import lax
from jax.experimental import pallas as pl
from jax.experimental.pallas import tpu as pltpu
from jax.sharding import PartitionSpec as P

HD = 128
HEADS = 32
KVH = 4
BLOCK = 128
GROUP = 16
ROWS = 32
SPAN = 512
CHUNKS = (3072, 3072, 2048)

NORM_EPS = 1e-05
SCALE_EPS = 1e-06
ROPE_BASE = 500000.0
F32 = jnp.float32
BF16 = jnp.bfloat16


def send(block, target):
    return lax.ppermute(block, "tensor", [(t, target(t)) for t in range(GROUP)])


def by_y(distance):
    return lambda t: (t & 9) | ((((t >> 1) + distance) & 3) << 1)


def by_z(t):
    return t ^ 8


def by_core(t):
    return t ^ 1


NEAR = [(0, 0), (0, 1), (0, 3), (1, 0)]
FAR = [(0, 2), (1, 1), (1, 3), (1, 2)]
ROWS_BY_ROWS = (((1,), (1,)), ((), ()))
NO_COST = pl.CostEstimate(flops=0, bytes_accessed=0, transcendentals=0)
VMEM = pl.BlockSpec(memory_space=pltpu.VMEM)
SMEM = pl.BlockSpec(memory_space=pltpu.SMEM)


def held_rows(position):
    z, y, core = position >> 3, (position >> 1) & 3, position & 1
    blocks = [
        ((z ^ dz) << 3) | (((y + dy) & 3) << 1) | (core ^ swap)
        for steps in (NEAR, FAR)
        for swap in (0, 1)
        for dz, dy in steps
    ]
    return (jnp.stack(blocks)[:, None] * ROWS + jnp.arange(ROWS, dtype=jnp.int32)).reshape(-1)


def hadamard(size):
    index = jnp.arange(size, dtype=jnp.int32)
    common = index[:, None] & index[None, :]
    parity = jnp.zeros((size, size), jnp.int32)
    for bit in range(size.bit_length() - 1):
        parity = parity + (common >> bit & 1)
    return jnp.where(parity % 2 == 0, 1.0, -1.0).astype(F32)


def call(kernel, shapes, inputs, scalars=(), behind=(), limit=12, scratch=()):
    count, waits = len(inputs), len(behind)
    specs = [SMEM if i in scalars else VMEM for i in range(count)]

    def body(*refs):
        kernel(*refs[:count], *refs[count + waits :])

    return pl.pallas_call(
        body,
        out_shape=shapes,
        in_specs=specs + [pl.BlockSpec(memory_space=pl.ANY)] * waits,
        out_specs=jax.tree.map(lambda _: VMEM, shapes),
        scratch_shapes=scratch,
        compiler_params=pltpu.CompilerParams(vmem_limit_bytes=limit << 20),
        cost_estimate=NO_COST,
    )(*inputs, *behind)


def shape(rows, columns, kind=BF16):
    return jax.ShapeDtypeStruct((rows, columns), kind)


def norm_kernel(x_ref, gain_ref, out_ref):
    values = x_ref[...].astype(F32)
    inverse = lax.rsqrt(jnp.mean(values * values, axis=1, keepdims=True) + NORM_EPS)
    out_ref[...] = (values * inverse * gain_ref[...]).astype(BF16)


def forward_kernel(own_ref, up_ref, down_ref, other_ref, to_down_ref, to_up_ref, to_z_ref, near_ref):
    full = own_ref.shape[1]
    half, quarter = full // 2, full // 4
    to_down_ref[:, :half] = up_ref[:, :half]
    to_down_ref[:, half:] = other_ref[:, :quarter]
    to_up_ref[:, :half] = down_ref[:, half:]
    to_up_ref[:, half:] = other_ref[:, :quarter]
    to_z_ref[:, : full - quarter] = up_ref[:, quarter:]
    to_z_ref[:, full - quarter :] = down_ref[:, quarter:]
    for place, ref in enumerate((own_ref, up_ref, down_ref, other_ref)):
        near_ref[place * ROWS : (place + 1) * ROWS, :] = ref[...]


def copy_kernel(in_ref, out_ref):
    out_ref[...] = in_ref[...]


def join_kernel(*refs):
    out_ref, at = refs[-1], 0
    for top, low in (refs[:2], refs[2:4]):
        rows, width = top.shape
        out_ref[:rows, at : at + width] = top[...]
        out_ref[rows:, at : at + width] = low[...]
        at += width


def near_kernel(step, mine_ref, theirs_ref, wq_ref, wkv_ref, q_ref, kv_ref):
    q = jnp.zeros(q_ref.shape, F32)
    kv = jnp.zeros(kv_ref.shape, F32)
    for start in range(0, wq_ref.shape[0], step):
        at = slice(start, start + step)
        rows = jnp.concatenate([mine_ref[:, at], theirs_ref[:, at]], axis=0)
        q += jnp.dot(rows, wq_ref[at, :], preferred_element_type=F32)
        kv += lax.dot_general(wkv_ref[:, at], rows, ROWS_BY_ROWS, preferred_element_type=F32)
    q_ref[...] = q
    kv_ref[...] = kv.astype(BF16)


def gathered(layout, pieces, start, step):
    parts = []
    for spans in layout:
        for which, low, high, base in spans:
            if low <= start < high:
                parts.append(pieces[which][:, base + start - low : base + start - low + step])
    return jnp.concatenate(parts, axis=0)


def far_keyval_kernel(layout, step, *refs):
    pieces, (wkv_ref, near_ref, order_ref, kv_ref) = refs[:-4], refs[-4:]
    kv = jnp.zeros(near_ref.shape, F32)
    for start in range(0, wkv_ref.shape[1], step):
        rows = gathered(layout, pieces, start, step)
        columns = wkv_ref[:, start : start + step]
        kv += lax.dot_general(columns, rows, ROWS_BY_ROWS, preferred_element_type=F32)
    both = jnp.concatenate([near_ref[...], kv.astype(BF16)], axis=1)
    kv_ref[...] = jnp.dot(both, order_ref[...], preferred_element_type=F32).astype(BF16)


def far_query_kernel(layout, step, *refs):
    pieces, (wq_ref, q_ref) = refs[:-2], refs[-2:]
    q = jnp.zeros(q_ref.shape, F32)
    for start in range(0, wq_ref.shape[0], step):
        rows = gathered(layout, pieces, start, step)
        q += jnp.dot(rows, wq_ref[start : start + step, :], preferred_element_type=F32)
    q_ref[...] = q


def pick(flags_ref, mine, theirs):
    half = mine.shape[0] // 2
    turned, core = flags_ref[0] != 0, flags_ref[1] != 0
    low = jnp.where(core, theirs, mine)
    high = jnp.where(core, mine, theirs)
    keys = jnp.concatenate(
        [jnp.where(turned, low[half:], low[:half]), jnp.where(turned, high[half:], high[:half])]
    )
    values = jnp.concatenate(
        [jnp.where(turned, low[:half], low[half:]), jnp.where(turned, high[:half], high[half:])]
    )
    return keys, values


TILE = 256


def attend_kernel(cached, flags_ref, qn_ref, qf_ref, row_ref, key_ref, mine_ref, theirs_ref, out_ref, joined_ref):
    keys, values = pick(flags_ref, mine_ref[...], theirs_ref[...])
    half = HD // 2
    first, second = keys[:half, cached:].astype(F32), keys[half:, cached:].astype(F32)
    cosine, sine = key_ref[:half, :], key_ref[half:, :]
    new_keys = jnp.concatenate(
        [first * cosine - second * sine, second * cosine + first * sine], axis=0
    ).astype(BF16)
    old_keys, old_values, new_values = keys[:, :cached], values[:, :cached], values[:, cached:]
    bias = jnp.where(
        lax.broadcasted_iota(jnp.int32, (1, cached), 1) < flags_ref[2], 0.0, -1e30
    )
    factor = 1.0 / math.sqrt(HD)
    for source, start in ((qn_ref, 0), (qf_ref, TILE)):
        at = slice(start, start + TILE)
        column = lax.broadcasted_iota(jnp.int32, (TILE, new_keys.shape[1]), 1)
        seen = column <= row_ref[at, 2 * HD : 2 * HD + 1].astype(jnp.int32)
        for head in range(2):
            columns = slice(head * HD, (head + 1) * HD)
            raw = source[:, columns]
            query = raw * row_ref[at, :HD] + pltpu.roll(raw, half, 1) * row_ref[at, HD : 2 * HD]
            query = query.astype(BF16)
            old = jnp.dot(query, old_keys, preferred_element_type=F32) * factor + bias
            new = jnp.dot(query, new_keys, preferred_element_type=F32) * factor
            new = jnp.where(seen, new, -1e30)
            top = jnp.maximum(
                jnp.max(old, axis=1, keepdims=True), jnp.max(new, axis=1, keepdims=True)
            )
            old, new = jnp.exp(old - top), jnp.exp(new - top)
            total = jnp.sum(old, axis=1, keepdims=True) + jnp.sum(new, axis=1, keepdims=True)
            value = lax.dot_general(
                old.astype(BF16), old_values, ROWS_BY_ROWS, preferred_element_type=F32
            )
            value += lax.dot_general(
                new.astype(BF16), new_values, ROWS_BY_ROWS, preferred_element_type=F32
            )
            joined_ref[at, columns] = (value / total).astype(BF16)
    for core in (0, 1):
        near, far = 4 * core, 8 + 4 * core
        order = (near, near + 3, near + 1, far + 1, near + 2, far + 2, far, far + 3)
        for place, block in enumerate(order):
            piece = joined_ref[block * ROWS : (block + 1) * ROWS, :]
            to = slice((8 * core + place) * ROWS, (8 * core + place + 1) * ROWS)
            out_ref[to, : 2 * HD] = piece
            out_ref[to, 2 * HD :] = piece


def turn_kernel(w_ref, table_ref, out_ref):
    rows = w_ref.shape[0]
    for start in range(0, w_ref.shape[1], 2 * BLOCK):
        at = slice(start, start + 2 * BLOCK)
        turned = jnp.dot(w_ref[:, at], table_ref[...], preferred_element_type=F32)
        turned = turned * (1.0 / math.sqrt(BLOCK))
        high = turned.astype(BF16)
        out_ref[:rows, at] = high
        out_ref[rows:, at] = (turned - high.astype(F32)).astype(BF16)


def turn_weights(w_out, table, start, width, behind, tile=512):
    rows = w_out.shape[0]
    return pl.pallas_call(
        lambda w_ref, table_ref, behind_ref, out_ref: turn_kernel(w_ref, table_ref, out_ref),
        grid=(width // tile,),
        in_specs=[
            pl.BlockSpec((rows, tile), lambda i: (0, start // tile + i)),
            pl.BlockSpec(table.shape, lambda i: (0, 0)),
            pl.BlockSpec(memory_space=pl.ANY),
        ],
        out_specs=pl.BlockSpec((2 * rows, tile), lambda i: (0, i)),
        out_shape=jax.ShapeDtypeStruct((2 * rows, width), BF16),
        compiler_params=pltpu.CompilerParams(vmem_limit_bytes=8 << 20),
        cost_estimate=NO_COST,
    )(w_out, table, behind)


def output_kernel(att_ref, w_ref, keep_ref, give_ref):
    half = keep_ref.shape[0]
    for start in range(0, w_ref.shape[1], 2 * BLOCK):
        pair = jnp.dot(
            att_ref[...], w_ref[:, start : start + 2 * BLOCK], preferred_element_type=F32
        )
        for at in range(0, 2 * BLOCK, BLOCK):
            block = pair[:, at : at + BLOCK]
            scale = jnp.max(jnp.abs(block), axis=1, keepdims=True) + SCALE_EPS
            level = (block * (1.0 / scale)).astype(BF16)
            value = (scale * level.astype(F32)).astype(BF16)
            columns = slice(start + at, start + at + BLOCK)
            keep_ref[:, columns] = value[:half]
            give_ref[:, columns] = value[half:]


def output_partial(attention, turned, behind=()):
    rows, width = attention.shape[0], turned.shape[1]
    half, waits = shape(rows // 2, width), len(behind)
    return pl.pallas_call(
        lambda *refs: output_kernel(*refs[:2], *refs[2 + waits :]),
        in_specs=[VMEM, VMEM] + [pl.BlockSpec(memory_space=pl.ANY)] * waits,
        out_specs=(VMEM, VMEM),
        out_shape=(half, half),
        compiler_params=pltpu.CompilerParams(vmem_limit_bytes=12 << 20),
        cost_estimate=pl.CostEstimate(
            flops=5000000 * width, bytes_accessed=0, transcendentals=0
        ),
    )(attention, turned, *behind)


def gather_head(block):
    got = []
    for turn in range(2):
        pairs = []
        for t in range(GROUP):
            head, chip, core = t >> 2, (t >> 1) & 1, t & 1
            pairs.append((8 * (chip ^ turn) + 2 * head + core, t))
        got.append(lax.ppermute(block, "tensor", pairs))
    return got


def add_kernel(keep_ref, got_ref, to_up_ref, to_down_ref, rest_ref):
    half = to_up_ref.shape[1] // 2
    left, right = slice(0, half), slice(half, 2 * half)

    def total(first, last, columns):
        return keep_ref[first:last, columns].astype(F32) + got_ref[first:last, columns].astype(F32)

    to_up_ref[:, left] = total(192, 256, left).astype(BF16)
    to_up_ref[:, right] = total(64, 128, right).astype(BF16)
    to_down_ref[:, left] = total(128, 192, left).astype(BF16)
    to_down_ref[:, right] = total(192, 256, right).astype(BF16)
    rest_ref[:64, left] = total(0, 64, left)
    rest_ref[:64, right] = total(0, 64, right)
    rest_ref[64:, left] = total(64, 128, left)
    rest_ref[64:, right] = total(128, 192, right)


def middle_kernel(rest_ref, from_down_ref, from_up_ref, to_up_ref, to_down_ref, near_ref):
    half = to_up_ref.shape[1]
    left, right = slice(0, half), slice(half, 2 * half)
    to_up_ref[...] = (rest_ref[64:, left] + from_down_ref[:, left].astype(F32)).astype(BF16)
    to_down_ref[...] = (rest_ref[64:, right] + from_up_ref[:, right].astype(F32)).astype(BF16)
    near_ref[:, left] = rest_ref[:64, left] + from_up_ref[:, left].astype(F32)
    near_ref[:, right] = rest_ref[:64, right] + from_down_ref[:, right].astype(F32)


def last_kernel(near_ref, from_down_ref, from_up_ref, mine_ref, to_z_ref):
    half = from_up_ref.shape[1]
    for at, ref in ((0, from_down_ref), (half, from_up_ref)):
        columns = slice(at, at + half)
        total = near_ref[:, columns] + ref[...].astype(F32)
        mine_ref[:, columns] = total[:32]
        to_z_ref[:, columns] = total[32:].astype(BF16)


def select_kernel(flags_ref, first_ref, second_ref, out_ref):
    out_ref[...] = jnp.where(flags_ref[3] != 0, first_ref[...], second_ref[...])


def layer_kernel(start, mine_ref, from_z_ref, hidden_ref, table_ref, out_ref):
    total = mine_ref[...] + from_z_ref[...].astype(F32)
    for at in range(0, total.shape[1], 2 * BLOCK):
        rest = total[:, at : at + 2 * BLOCK]
        restored = jnp.zeros(rest.shape, F32)
        for _ in range(3):
            part = rest.astype(BF16)
            restored += jnp.dot(part, table_ref[...], preferred_element_type=F32)
            rest = rest - part.astype(F32)
        before = hidden_ref[:, start + at : start + at + 2 * BLOCK].astype(F32)
        out_ref[:, at : at + 2 * BLOCK] = (before + restored * (1.0 / math.sqrt(BLOCK))).astype(BF16)


def local(hidden, gain, w_query, w_keyval, w_out, cache_kv, offsets):
    position = lax.axis_index("tensor")
    offset = offsets[0]
    full = w_query.shape[0]
    normed = call(norm_kernel, shape(*hidden.shape), (hidden, gain))

    up = send(normed, by_y(-1))
    down = send(normed, by_y(1))
    other = send(normed, by_z)

    held = held_rows(position)
    span = jnp.arange(SPAN, dtype=jnp.int32)
    order = (held[:, None] == span[None, :]).astype(BF16)
    freqs = ROPE_BASE ** (-(2.0 / HD) * jnp.arange(HD // 2, dtype=F32))
    angles = (offset + held).astype(F32)[:, None] * freqs[None, :]
    cosine, sine = jnp.cos(angles), jnp.sin(angles)
    index = jnp.broadcast_to(held.astype(F32)[:, None], (SPAN, HD))
    row_table = jnp.concatenate([cosine, cosine, -sine, sine, index], axis=1)
    angles = freqs[:, None] * (offset + span).astype(F32)[None, :]
    key_table = jnp.concatenate([jnp.cos(angles), jnp.sin(angles)], axis=0)
    section = lax.axis_index("section")
    edge = (section & 3) == 0
    flags = jnp.stack([(position >> 1) & 1, position & 1, offset, edge]).astype(jnp.int32)
    table = hadamard(BLOCK)
    zero = jnp.zeros_like(table)
    pair = jnp.concatenate(
        [jnp.concatenate([table, zero], axis=1), jnp.concatenate([zero, table], axis=1)], axis=0
    ).astype(BF16)
    starts = [sum(CHUNKS[:i]) for i in range(len(CHUNKS))]

    half, quarter = full // 2, full // 4
    to_down, to_up, to_z, near = call(
        forward_kernel,
        (shape(ROWS, half + quarter), shape(ROWS, half + quarter), shape(ROWS, 2 * (full - quarter)), shape(4 * ROWS, full)),
        (normed, up, down, other),
        behind=(order, row_table, key_table, pair),
    )
    from_up = send(to_down, by_y(-1))
    from_down = send(to_up, by_y(1))
    from_z = send(to_z, by_z)
    far = send(other, by_y(2))
    near_theirs = send(near, by_core)
    turned = [turn_weights(w_out, pair, at, width, to_z) for at, width in zip(starts, CHUNKS)]
    layout = []
    for base in (0, 4):
        layout += [
            [(base, 0, half, 0), (base + 1, half, full, 0)],
            [(base, 0, quarter, half), (base + 2, quarter, full, 0)],
            [(base + 1, 0, quarter, half), (base + 2, quarter, full, full - quarter)],
            [(base + 3, 0, full, 0)],
        ]
    query_width, kv_width = w_query.shape[1], w_keyval.shape[1]
    rows, cached = SPAN // 2, cache_kv.shape[0]
    q_near, kv_near = call(
        functools.partial(near_kernel, 1024),
        (shape(rows, query_width, F32), shape(kv_width, rows)),
        (near, near_theirs, w_query, w_keyval.T),
        behind=turned,
    )
    distant = [from_up, from_down, from_z, far]
    cache = call(copy_kernel, shape(kv_width, cached), (cache_kv.T,), behind=distant)
    from_z = call(copy_kernel, shape(*from_z.shape), (from_z,), behind=(kv_near,))
    distant = distant + [send(piece, by_core) for piece in (from_up, from_down, from_z, far)]
    cache = gather_head(cache)
    keyval = call(
        functools.partial(far_keyval_kernel, layout, 1024),
        shape(kv_width, SPAN),
        (*distant, w_keyval.T, kv_near, order),
    )
    new = gather_head(keyval)
    q_far = call(
        functools.partial(far_query_kernel, layout, 1024),
        shape(rows, query_width, F32),
        (*distant, w_query),
        behind=(keyval,),
    )
    mine = call(join_kernel, shape(2 * kv_width, cached + SPAN), (*cache, *new), behind=(q_far,))
    attention = call(
        functools.partial(attend_kernel, cached),
        shape(SPAN, 2 * query_width),
        (flags, q_near, q_far, row_table, key_table, mine, send(mine, by_core)),
        scalars=(0,),
        limit=16,
        scratch=[pltpu.VMEM((SPAN, query_width), BF16)],
    )

    sections = lax.axis_size("section")
    route = [(i, (i + 1) % sections) for i in range(sections)]
    along_x = [(i, (i & ~3) | ((i + 1) & 3)) for i in range(sections)]
    along_z = [(i, (i + 4) % sections) for i in range(0, sections, 4)]

    def hand_on(block, around=None):
        if around is None:
            return lax.ppermute(block, "section", route)
        beside = lax.ppermute(block, "section", along_x)
        above = lax.ppermute(beside, "section", along_z)
        return call(
            select_kernel, shape(*block.shape), (flags, above, beside), scalars=(0,), behind=around
        )

    rests, nears, first, second, layers, results = [], [], [], [], [], []

    def project_out(chunk, behind=()):
        keep, give = output_partial(attention, turned[chunk], behind)
        return CHUNKS[chunk], keep, give

    def round_1(width, keep, give, behind=()):
        to_up, to_down, rest = call(
            add_kernel,
            (shape(64, width), shape(64, width), shape(128, width, F32)),
            (keep, send(give, by_core)),
            behind=behind,
        )
        rests.append(rest)
        first.append((send(to_up, by_y(1)), send(to_down, by_y(-1))))

    def round_2(chunk, behind=()):
        width = CHUNKS[chunk]
        to_up, to_down, near = call(
            middle_kernel,
            (shape(64, width // 2), shape(64, width // 2), shape(64, width, F32)),
            (rests[chunk], *first[chunk]),
            behind=behind,
        )
        nears.append(near)
        second.append((send(to_up, by_y(1)), send(to_down, by_y(-1))))

    def round_3(chunk, behind=(), behind_last=()):
        width = CHUNKS[chunk]
        mine, to_z = call(
            last_kernel,
            (shape(32, width, F32), shape(32, width)),
            (nears[chunk], *second[chunk]),
            behind=behind,
        )
        layers.append(
            call(
                functools.partial(layer_kernel, starts[chunk]),
                shape(32, width),
                (mine, send(to_z, by_z), hidden, pair),
                behind=behind_last,
            )
        )
        results.append(hand_on(layers[chunk], () if chunk == 1 else None))

    parts = []
    for chunk in range(3):
        parts.append(project_out(chunk, (parts[-1][1],) if parts else ()))
    for chunk in range(3):
        round_1(*parts[chunk])
    round_2(0)
    round_3(0)
    round_2(1)
    round_3(1)
    round_2(2, (layers[0],))
    round_3(2, (layers[1],), (results[0],))
    return jnp.concatenate(results, axis=1)


def solution(mesh):
    placed = (
        P(("section", "tensor"), None),
        P("section", None),
        P("section", "tensor"),
        P("section", "tensor"),
        P(("section", "tensor"), None),
        P("section", "tensor"),
        P("section"),
    )
    return jax.shard_map(
        local, mesh=mesh, in_specs=placed, out_specs=P(("section", "tensor"), None), check_vma=False
    )
```
